256 devices in a mesh: section: 32 (over y, z_lo, core), dp: 8 (over x, z_hi).
Axes of the slice: x: 4, y: 4, z: 8 (z_hi: 2, z_lo: 4; z = z_hi * 4 + z_lo), core: 2. Of those that a mesh axis runs over, the one named last changes fastest.
Arguments:
- section_states: bfloat16 [32, 4, 8, 16, 16, 512], P('section', None, 'dp'), may hold values from -6 to 6
- conv_kernels: bfloat16 [32, 2, 1152, 512], P('section'), may hold values from -0.1875 to 0.1875
- top_feed: bfloat16 [3, 4, 8, 16, 16, 512], P(None, None, 'dp'), may hold values from -6 to 6
Outputs:
- final_states: bfloat16 [32, 4, 8, 16, 16, 512], P('section', None, 'dp')
- kernel_grads: float32 [32, 2, 1152, 512], P('section', None, 'dp')
The draws below stay inside these ranges and needn't reach their ends.
All inputs are finite; a program needn't handle non-finite values.
Results may differ from the reference program's by a relative error of at most 0.024.
Values may be sent and summed in bfloat16 or wider, within the bound.
No kernel may reach another device: no remote copies, remote signals or barrier semaphores. Data moves between devices by JAX's collectives and lax.ppermute only.
A program may use at most 128 MiB of HBM per device.

```python
import jax
import jax.numpy as jnp
from jax import lax

CH = 512
GW = 128
HW = 16
TICKS = 4
IMAGES = 8
SECTIONS = 32


def steps_of(rng, extent, split, least, largest):
    def one(axis_at, shards_of):
        heights = jax.random.uniform(jax.random.fold_in(jax.random.fold_in(rng, 6), axis_at), (shards_of,), jnp.float32, least / len(split), largest / len(split))
        return jnp.repeat(jnp.exp(heights), extent[axis_at] // shards_of).reshape((-1,) + (1,) * (len(extent) - axis_at - 1))

    level = one(*split[0])
    for cut in split[1:]:
        level = level * one(*cut)
    return level


def bell_draw(own_key, dims, deviation, bound, cuts=(), held_as=jnp.bfloat16):
    factor_of = steps_of(own_key, dims, cuts, -0.22, 0.18) if cuts else 1.0
    entries = jax.random.normal(own_key, dims, jnp.float32) * deviation * factor_of
    return jnp.minimum(jnp.maximum(entries, -bound), bound).astype(held_as)


def setup_inputs(seed: int = 0) -> dict:
    keys = jax.random.split(jax.random.key(seed), 4)
    return {
        "section_states": bell_draw(keys[0], (SECTIONS, 4, IMAGES, HW, HW, CH), 1.0, 6.0, ((0, 32), (2, 8))),
        "conv_kernels": bell_draw(keys[1], (SECTIONS, 2, 9 * GW, CH), (9 * GW) ** -0.5, 0.1875, ((0, 32),)),
        "top_feed": bell_draw(keys[2], (TICKS - 1, 4, IMAGES, HW, HW, CH), 1.0, 6.0, ((2, 8),)),
    }


def tap_stack(field):
    height = field.shape[1]
    width = field.shape[2]
    padded = jnp.pad(field, ((0, 0), (1, 1), (1, 1), (0, 0)))
    pieces = [padded[:, row_off:row_off + height, col_off:col_off + width, :] for row_off in range(3) for col_off in range(3)]
    stacked = jnp.stack(pieces, axis=3)
    return stacked.reshape(field.shape[0] * height * width, 9, field.shape[3] // GW, GW)

def smooth_grad(value):
    sigma = jax.nn.sigmoid(value)
    return sigma * (1.0 + value * (1.0 - sigma))

def kernel_view(kernel):
    return kernel.reshape(9, GW, kernel.shape[1] // GW, GW).astype(jnp.float32)

def conv_apply(taps, kernel, shape):
    result = jnp.einsum('nkgi,kigo->ngo', taps.astype(jnp.float32), kernel_view(kernel))
    return result.reshape(shape)

def conv_back(grad_field, kernel):
    taps = tap_stack(grad_field)[:, ::-1]
    result = jnp.einsum('nkgo,kigo->ngi', taps.astype(jnp.float32), kernel_view(kernel))
    return result.reshape(grad_field.shape)

def kernel_term(taps, grad_field):
    count = taps.shape[0]
    flat = grad_field.reshape(count, taps.shape[2], GW).astype(jnp.float32)
    result = jnp.einsum('nkgi,ngo->kigo', taps.astype(jnp.float32), flat)
    return result.reshape(9 * GW, taps.shape[2] * GW)

def coupling_back(state, kernels):
    shape = state.shape[1:]
    output_one = state[0].astype(jnp.float32)
    output_two = state[1].astype(jnp.float32)
    grad_one = state[2]
    grad_two = state[3]
    act_one = jax.nn.silu(output_one).astype(jnp.bfloat16)
    taps_one = tap_stack(act_one)
    input_two = (output_two - conv_apply(taps_one, kernels[1], shape)).astype(jnp.bfloat16)
    wide_two = input_two.astype(jnp.float32)
    act_two = jax.nn.silu(wide_two).astype(jnp.bfloat16)
    taps_two = tap_stack(act_two)
    input_one = (output_one - conv_apply(taps_two, kernels[0], shape)).astype(jnp.bfloat16)
    total_one = (grad_one.astype(jnp.float32) + conv_back(grad_two, kernels[1]) * smooth_grad(output_one)).astype(jnp.bfloat16)
    term_second = kernel_term(taps_one, grad_two)
    grad_input_two = (grad_two.astype(jnp.float32) + conv_back(total_one, kernels[0]) * smooth_grad(wide_two)).astype(jnp.bfloat16)
    term_first = kernel_term(taps_two, total_one)
    return (jnp.stack([input_one, input_two, total_one, grad_input_two]), jnp.stack([term_first, term_second]))

def run_section(pair):
    return coupling_back(pair[0], pair[1])

def reference(section_states, conv_kernels, top_feed):
    current = section_states
    total = jnp.zeros(conv_kernels.shape, jnp.float32)
    produced = section_states
    for tick in range(TICKS):
        produced, grads = lax.map(run_section, (current, conv_kernels))
        total = total + grads
        if tick + 1 < TICKS:
            current = jnp.concatenate([produced[1:], top_feed[tick][None]], axis=0)
    return (produced, total * (1.0 / (HW * HW)))
```

```python
import functools

import jax
import jax.numpy as jnp
from jax import lax
from jax.experimental import pallas as pl
from jax.experimental.pallas import tpu as pltpu
from jax.sharding import Mesh
from jax.sharding import PartitionSpec as P

GW = 128
HW = 16
TICKS = 4
CELLS = HW * HW
ROWS = 9 * GW
HALVES = 2
VMEM_LIMIT = 24 * 1024 * 1024


def column_shifts(field, at_left, at_right):
    before = jnp.where(at_left, 0.0, pltpu.roll(field, 1, 0))
    after = jnp.where(at_right, 0.0, pltpu.roll(field, CELLS - 1, 0))
    return jnp.concatenate(
        [before.astype(jnp.bfloat16), field.astype(jnp.bfloat16), after.astype(jnp.bfloat16)], axis=1
    )


def row_shifts(field):
    edge = jnp.zeros((HW, GW), field.dtype)
    up = jnp.concatenate([field[HW:], edge], axis=0)
    down = jnp.concatenate([edge, field[:-HW]], axis=0)
    return jnp.concatenate([up, field, down], axis=1)


def taps_by_row(kernel_ref, branch, lanes):
    return jnp.concatenate(
        [kernel_ref[branch, pl.ds(a * 3 * GW, 3 * GW), lanes] for a in range(3)], axis=1
    )


def conv(stack, kernel):
    parts = jnp.dot(stack, kernel, preferred_element_type=jnp.float32)
    edge = jnp.zeros((HW, GW), jnp.float32)
    above = jnp.concatenate([edge, parts[:-HW, :GW]], axis=0)
    below = jnp.concatenate([parts[HW:, 2 * GW :], edge], axis=0)
    return parts[:, GW : 2 * GW] + above + below


def conv_back(stack, kernel, at_left, at_right):
    parts = lax.dot_general(
        stack, kernel, (((1,), (1,)), ((), ())), preferred_element_type=jnp.float32
    )
    before = jnp.where(at_right, 0.0, pltpu.roll(parts[:, :GW], CELLS - 1, 0))
    after = jnp.where(at_left, 0.0, pltpu.roll(parts[:, 2 * GW :], 1, 0))
    return parts[:, GW : 2 * GW] + before + after


def correlate(columns, rows):
    return lax.dot_general(
        columns, rows, (((0,), (0,)), ((), ())), preferred_element_type=jnp.float32
    )


def masks():
    column = lax.rem(lax.broadcasted_iota(jnp.int32, (CELLS, GW), 0), HW)
    return column == 0, column == HW - 1


def section_back(state_ref, lanes, kernel_g, kernel_f, store, keep):
    edges = masks()
    grad_two = state_ref[3, :, lanes]
    out_one = state_ref[0, :, lanes].astype(jnp.float32)
    sigma_one = jax.nn.sigmoid(out_one)
    slope_one = sigma_one * (1.0 + out_one * (1.0 - sigma_one))
    act_one = out_one * sigma_one
    columns_one = column_shifts(act_one, *edges)
    rows_two = row_shifts(grad_two)

    weights = kernel_g()
    in_two = (state_ref[1, :, lanes].astype(jnp.float32) - conv(columns_one, weights)).astype(
        jnp.bfloat16
    )
    total_one = (
        state_ref[2, :, lanes].astype(jnp.float32)
        + conv_back(rows_two, weights, *edges) * slope_one
    ).astype(jnp.bfloat16)
    rows_one = row_shifts(total_one)

    wide_two = in_two.astype(jnp.float32)
    sigma_two = jax.nn.sigmoid(wide_two)
    slope_two = sigma_two * (1.0 + wide_two * (1.0 - sigma_two))
    act_two = wide_two * sigma_two
    columns_two = column_shifts(act_two, *edges)

    weights = kernel_f()
    in_one = (out_one - conv(columns_two, weights)).astype(jnp.bfloat16)
    total_two = (
        grad_two.astype(jnp.float32) + conv_back(rows_one, weights, *edges) * slope_two
    ).astype(jnp.bfloat16)
    for at, stream in enumerate((in_one, in_two, total_one, total_two)):
        store(at, stream)
    keep(act_one, act_two, grad_two, total_one, columns_one, columns_two, rows_two, rows_one)


def group_lanes(group):
    return pl.ds(group * GW, GW)


def kernel_loads(half, width, kernels, held, sems):
    copies = {}
    for group in range(width // GW):
        wide = pl.ds(half * width + group * GW, GW)
        for branch in (1, 0):
            copies[group, branch] = pltpu.make_async_copy(
                kernels.at[branch, :, wide],
                held.at[branch, :, group_lanes(group)],
                sems.at[branch, group],
            )
            copies[group, branch].start()

    def loaded(group, branch):
        copies[group, branch].wait()
        return taps_by_row(held, branch, group_lanes(group))

    return loaded


def take_top(is_top, tick, half, width, top, made, sem):
    @pl.when(is_top[0] == 1)
    def _():
        copy = pltpu.make_async_copy(
            top.at[tick - 1, :, :, pl.ds(half * width, width)], made, sem
        )
        copy.start()
        copy.wait()


def early_tick(tick, half, width, *refs):
    if tick:
        is_top, received, top, kernels, earlier, made, kept, turn, held, sent, sems, sem, out_sems = refs
    else:
        states, kernels, earlier, made, kept, turn, held, sent, sems, sem, out_sems = refs
    if not tick:
        copies = []
        for group in range(width // GW):
            lanes = group_lanes(group)
            wide = pl.ds(half * width + group * GW, GW)
            copies.append(
                pltpu.make_async_copy(states.at[:, :, wide], made.at[:, :, lanes], sem.at[group])
            )
            copies[-1].start()
    loaded = kernel_loads(half, width, kernels, held, sems)
    turn[...] = jnp.zeros_like(turn)
    if tick:
        take_top(is_top, tick, half, width, top, made, sem.at[0])
    outgoing = []
    for group in range(width // GW):
        lanes = group_lanes(group)
        if not tick:
            copies[group].wait()

        def store(at, stream):
            made[at, :, lanes] = stream

        def keep(act_one, act_two, grad_two, total_one, *stacks):
            sent[0, :, lanes] = act_two.astype(jnp.bfloat16)
            sent[1, :, lanes] = act_one.astype(jnp.bfloat16)
            sent[2, :, lanes] = total_one
            sent[3, :, lanes] = grad_two
            copy = pltpu.make_async_copy(
                sent.at[:, :, lanes], kept.at[:, :, lanes], out_sems.at[group]
            )
            copy.start()
            outgoing.append(copy)

        section_back(
            made,
            lanes,
            functools.partial(loaded, group, 1),
            functools.partial(loaded, group, 0),
            store,
            keep,
        )
    for copy in outgoing:
        copy.wait()


def early_terms(width, *refs):
    kept = refs[: TICKS - 1]
    earlier, total, turn, fields, summed, sems, out_sems = refs[TICKS - 1 :]
    turn[...] = jnp.zeros_like(turn)
    edges = masks()
    copies = {}
    for group in range(width // GW):
        lanes = group_lanes(group)
        for tick in range(TICKS - 1):
            copies[group, tick] = pltpu.make_async_copy(
                kept[tick].at[:, :, lanes], fields.at[tick, :, :, lanes], sems.at[tick, group]
            )
            copies[group, tick].start()
    outgoing = []
    for group in range(width // GW):
        lanes = group_lanes(group)
        for tick in range(TICKS - 1):
            copies[group, tick].wait()
        for branch in range(2):
            columns = jnp.concatenate(
                [
                    column_shifts(fields[tick, branch, :, lanes].astype(jnp.float32), *edges)
                    for tick in range(TICKS - 1)
                ],
                axis=0,
            )
            rows = jnp.concatenate(
                [row_shifts(fields[tick, 2 + branch, :, lanes]) for tick in range(TICKS - 1)], axis=0
            )
            term = correlate(columns, rows)
            for a in range(3):
                summed[branch, pl.ds(a * 3 * GW, 3 * GW), lanes] = term[:, a * GW : (a + 1) * GW]
            copy = pltpu.make_async_copy(
                summed.at[branch, :, lanes], total.at[branch, :, lanes], out_sems.at[branch, group]
            )
            copy.start()
            outgoing.append(copy)
    for copy in outgoing:
        copy.wait()


def last_tick(half, width, is_top, received, top, kernels, total, earlier, *rest):
    made, final, share, turn, held, summed, sent, sems, sem, total_sem, final_sem, share_sems = rest[-12:]
    loaded = kernel_loads(half, width, kernels, held, sems)
    total_copy = pltpu.make_async_copy(total, summed, total_sem)
    total_copy.start()
    turn[...] = jnp.zeros_like(turn)
    take_top(is_top, TICKS - 1, half, width, top, made, sem)
    outgoing = []
    for group in range(width // GW):
        lanes = group_lanes(group)

        def store(at, stream):
            made[at, :, lanes] = stream

        def keep(act_one, act_two, grad_two, total_one, columns_one, columns_two, rows_two, rows_one):
            if not group:
                total_copy.wait()
            for branch, pair in ((1, (columns_one, rows_two)), (0, (columns_two, rows_one))):
                term = correlate(*pair)
                for a in range(3):
                    rows = pl.ds(a * 3 * GW, 3 * GW)
                    sent[branch, rows, lanes] = (
                        summed[branch, rows, lanes] + term[:, a * GW : (a + 1) * GW]
                    ).astype(jnp.bfloat16)
                copy = pltpu.make_async_copy(
                    sent.at[branch, :, lanes], share.at[branch, :, lanes], share_sems.at[branch, group]
                )
                copy.start()
                outgoing.append(copy)

        section_back(
            made,
            lanes,
            functools.partial(loaded, group, 1),
            functools.partial(loaded, group, 0),
            store,
            keep,
        )
    copy = pltpu.make_async_copy(made, final.at[:, :, pl.ds(half * width, width)], final_sem)
    copy.start()
    outgoing.append(copy)
    for copy in outgoing:
        copy.wait()


ANY_REF = pl.BlockSpec(memory_space=pl.ANY)
VMEM_REF = pl.BlockSpec(memory_space=pltpu.VMEM)
SMEM_REF = pl.BlockSpec(memory_space=pltpu.SMEM)


def in_vmem(array):
    return pltpu.with_memory_space_constraint(array, pltpu.VMEM)


def in_hbm(array):
    return pltpu.with_memory_space_constraint(array, pltpu.HBM)


def params():
    return pltpu.CompilerParams(vmem_limit_bytes=VMEM_LIMIT)


def cost(products, width):
    groups = width // GW
    return pl.CostEstimate(
        flops=products * 2 * CELLS * ROWS * GW * groups,
        bytes_accessed=4 * 4 * CELLS * width,
        transcendentals=2 * CELLS * width,
    )


def passed_down(value):
    count = lax.axis_size("section")
    return lax.ppermute(value, "section", [(source, source - 1) for source in range(1, count)])


def on_device(section_states, conv_kernels, top_feed):
    chans = section_states.shape[-1]
    width = chans // HALVES
    states = in_hbm(section_states.reshape(4, CELLS, chans))
    kernels = in_hbm(conv_kernels[0])
    top = in_hbm(top_feed.reshape(TICKS - 1, 4, CELLS, chans))
    is_top = (lax.axis_index("section") == lax.axis_size("section") - 1).astype(jnp.int32)[None]

    groups = width // GW
    state_type = pltpu.VMEM((4, CELLS, width), jnp.bfloat16)
    kept_type = pltpu.HBM((4, CELLS, width), jnp.bfloat16)
    turn_type = pltpu.VMEM((8, 128), jnp.float32)
    held_scratch = pltpu.VMEM((2, ROWS, width), jnp.bfloat16)
    turn = jnp.zeros((8, 128), jnp.float32)
    made, kept = [None] * HALVES, [[] for _ in range(HALVES)]
    for tick in range(TICKS - 1):
        for half in range(HALVES):
            operands, specs = [states, kernels, turn], [ANY_REF] * 3
            if tick:
                operands = [is_top, in_vmem(made[half]), top, kernels, turn]
                specs = [SMEM_REF, VMEM_REF, ANY_REF, ANY_REF, ANY_REF]
            out, fields, turn = pl.pallas_call(
                functools.partial(early_tick, tick, half, width),
                out_shape=(state_type, kept_type, turn_type),
                in_specs=specs,
                out_specs=(VMEM_REF, ANY_REF, VMEM_REF),
                scratch_shapes=[
                    held_scratch,
                    pltpu.VMEM((4, CELLS, width), jnp.bfloat16),
                    pltpu.SemaphoreType.DMA((2, groups)),
                    pltpu.SemaphoreType.DMA((groups,)),
                    pltpu.SemaphoreType.DMA((groups,)),
                ],
                input_output_aliases={1: 0} if tick else {},
                compiler_params=params(),
                cost_estimate=cost(4, width),
                name=f"tick_{tick}_{half}",
            )(*operands)
            made[half] = passed_down(out)
            kept[half].append(in_hbm(fields))

    total = []
    for half in range(HALVES):
        summed, turn = pl.pallas_call(
            functools.partial(early_terms, width),
            out_shape=(pltpu.HBM((2, ROWS, width), jnp.float32), turn_type),
            in_specs=[ANY_REF] * TICKS,
            out_specs=(ANY_REF, VMEM_REF),
            scratch_shapes=[
                pltpu.VMEM((TICKS - 1, 4, CELLS, width), jnp.bfloat16),
                pltpu.VMEM((2, ROWS, width), jnp.float32),
                pltpu.SemaphoreType.DMA((TICKS - 1, groups)),
                pltpu.SemaphoreType.DMA((2, groups)),
            ],
            compiler_params=params(),
            cost_estimate=cost(2 * (TICKS - 1), width),
            name=f"early_terms_{half}",
        )(*kept[half], turn)
        total.append(in_hbm(summed))

    final = None
    shares = []
    for half in range(HALVES):
        operands = [is_top, in_vmem(made[half]), top, kernels, total[half], turn]
        specs = [SMEM_REF, VMEM_REF, ANY_REF, ANY_REF, ANY_REF, ANY_REF]
        aliases = {1: 0}
        if half:
            operands.append(in_hbm(final))
            specs.append(ANY_REF)
            aliases[6] = 1
        _, final, share, turn = pl.pallas_call(
            functools.partial(last_tick, half, width),
            out_shape=(
                state_type,
                pltpu.HBM((4, CELLS, chans), jnp.bfloat16),
                pltpu.HBM((2, ROWS, width), jnp.bfloat16),
                turn_type,
            ),
            in_specs=specs,
            out_specs=(VMEM_REF, ANY_REF, ANY_REF, VMEM_REF),
            scratch_shapes=[
                held_scratch,
                pltpu.VMEM((2, ROWS, width), jnp.float32),
                pltpu.VMEM((2, ROWS, width), jnp.bfloat16),
                pltpu.SemaphoreType.DMA((2, groups)),
                pltpu.SemaphoreType.DMA(()),
                pltpu.SemaphoreType.DMA(()),
                pltpu.SemaphoreType.DMA(()),
                pltpu.SemaphoreType.DMA((2, groups)),
            ],
            input_output_aliases=aliases,
            compiler_params=params(),
            cost_estimate=cost(6, width),
            name=f"last_tick_{half}",
        )(*operands)
        for axis in ("dp_0", "dp_1"):
            share = lax.psum_scatter(share, axis, scatter_dimension=1, tiled=True)
        shares.append(share)
    grads = jnp.concatenate(shares, axis=2).astype(jnp.float32) * (1.0 / (HW * HW))
    return (final.reshape(1, 4, 1, HW, HW, chans), grads[None])


def solution(mesh):
    finer = Mesh(mesh.devices.reshape(mesh.shape["section"], 4, 2), ("section", "dp_0", "dp_1"))
    images = ("dp_0", "dp_1")
    in_specs = (
        P("section", None, images, None, None, None),
        P("section", None, None, None),
        P(None, None, images, None, None, None),
    )
    out_specs = (P("section", None, images, None, None, None), P("section", None, images, None))
    return jax.shard_map(
        on_device, mesh=finer, in_specs=in_specs, out_specs=out_specs, check_vma=False
    )
```

```python
import functools

import jax
import jax.numpy as jnp
from jax import lax
from jax.experimental import pallas as pl
from jax.experimental.pallas import tpu as pltpu
from jax.sharding import Mesh
from jax.sharding import PartitionSpec as P

GW = 128
HW = 16
TICKS = 4
CELLS = HW * HW
ROWS = 9 * GW
SHARE = ROWS // 8
HALVES = 2
VMEM_LIMIT = 24 * 1024 * 1024


def column_shifts(field, at_left, at_right):
    before = jnp.where(at_left, 0.0, pltpu.roll(field, 1, 0))
    after = jnp.where(at_right, 0.0, pltpu.roll(field, CELLS - 1, 0))
    return jnp.concatenate(
        [before.astype(jnp.bfloat16), field.astype(jnp.bfloat16), after.astype(jnp.bfloat16)], axis=1
    )


def row_shifts(field):
    edge = jnp.zeros((HW, GW), field.dtype)
    up = jnp.concatenate([field[HW:], edge], axis=0)
    down = jnp.concatenate([edge, field[:-HW]], axis=0)
    return jnp.concatenate([up, field, down], axis=1)


def taps_by_row(kernel_ref, branch, lanes):
    return jnp.concatenate(
        [kernel_ref[branch, pl.ds(a * 3 * GW, 3 * GW), lanes] for a in range(3)], axis=1
    )


def conv(stack, kernel):
    parts = jnp.dot(stack, kernel, preferred_element_type=jnp.float32)
    edge = jnp.zeros((HW, GW), jnp.float32)
    above = jnp.concatenate([edge, parts[:-HW, :GW]], axis=0)
    below = jnp.concatenate([parts[HW:, 2 * GW :], edge], axis=0)
    return parts[:, GW : 2 * GW] + above + below


def conv_back(stack, kernel, at_left, at_right):
    parts = lax.dot_general(
        stack, kernel, (((1,), (1,)), ((), ())), preferred_element_type=jnp.float32
    )
    before = jnp.where(at_right, 0.0, pltpu.roll(parts[:, :GW], CELLS - 1, 0))
    after = jnp.where(at_left, 0.0, pltpu.roll(parts[:, 2 * GW :], 1, 0))
    return parts[:, GW : 2 * GW] + before + after


def correlate(columns, rows):
    return lax.dot_general(
        columns, rows, (((0,), (0,)), ((), ())), preferred_element_type=jnp.float32
    )


def masks():
    column = lax.rem(lax.broadcasted_iota(jnp.int32, (CELLS, GW), 0), HW)
    return column == 0, column == HW - 1


def section_back(state_ref, lanes, kernel_g, kernel_f, store, keep):
    edges = masks()
    grad_two = state_ref[3, :, lanes]
    out_one = state_ref[0, :, lanes].astype(jnp.float32)
    sigma_one = jax.nn.sigmoid(out_one)
    slope_one = sigma_one * (1.0 + out_one * (1.0 - sigma_one))
    act_one = out_one * sigma_one
    columns_one = column_shifts(act_one, *edges)
    rows_two = row_shifts(grad_two)

    weights = kernel_g()
    in_two = (state_ref[1, :, lanes].astype(jnp.float32) - conv(columns_one, weights)).astype(
        jnp.bfloat16
    )
    total_one = (
        state_ref[2, :, lanes].astype(jnp.float32)
        + conv_back(rows_two, weights, *edges) * slope_one
    ).astype(jnp.bfloat16)
    rows_one = row_shifts(total_one)

    wide_two = in_two.astype(jnp.float32)
    sigma_two = jax.nn.sigmoid(wide_two)
    slope_two = sigma_two * (1.0 + wide_two * (1.0 - sigma_two))
    act_two = wide_two * sigma_two
    columns_two = column_shifts(act_two, *edges)

    weights = kernel_f()
    in_one = (out_one - conv(columns_two, weights)).astype(jnp.bfloat16)
    total_two = (
        grad_two.astype(jnp.float32) + conv_back(rows_one, weights, *edges) * slope_two
    ).astype(jnp.bfloat16)
    for at, stream in enumerate((in_one, in_two, total_one, total_two)):
        store(at, stream)
    keep(act_one, act_two, grad_two, total_one, columns_one, columns_two, rows_two, rows_one)


def group_lanes(group):
    return pl.ds(group * GW, GW)


def kernel_loads(half, width, kernels, held, sems):
    copies = {}
    for group in range(width // GW):
        wide = pl.ds(half * width + group * GW, GW)
        for branch in (1, 0):
            copies[group, branch] = pltpu.make_async_copy(
                kernels.at[branch, :, wide],
                held.at[branch, :, group_lanes(group)],
                sems.at[branch, group],
            )
            copies[group, branch].start()

    def loaded(group, branch):
        copies[group, branch].wait()
        return taps_by_row(held, branch, group_lanes(group))

    return loaded


def take_top(places, tick, half, width, top, made, sem):
    @pl.when(places[0] == 1)
    def _():
        copy = pltpu.make_async_copy(
            top.at[tick - 1, :, :, pl.ds(half * width, width)], made, sem
        )
        copy.start()
        copy.wait()


def early_tick(tick, half, width, *refs):
    if tick:
        places, received, top, kernels, earlier, made, kept, turn, held, sent, sems, sem, out_sems = refs
    else:
        states, kernels, earlier, made, kept, turn, held, sent, sems, sem, out_sems = refs
    if not tick:
        copies = []
        for group in range(width // GW):
            lanes = group_lanes(group)
            wide = pl.ds(half * width + group * GW, GW)
            copies.append(
                pltpu.make_async_copy(states.at[:, :, wide], made.at[:, :, lanes], sem.at[group])
            )
            copies[-1].start()
    loaded = kernel_loads(half, width, kernels, held, sems)
    turn[...] = jnp.zeros_like(turn)
    if tick:
        take_top(places, tick, half, width, top, made, sem.at[0])
    outgoing = []
    for group in range(width // GW):
        lanes = group_lanes(group)
        if not tick:
            copies[group].wait()

        def store(at, stream):
            made[at, :, lanes] = stream

        def keep(act_one, act_two, grad_two, total_one, *stacks):
            sent[0, :, lanes] = act_two.astype(jnp.bfloat16)
            sent[1, :, lanes] = act_one.astype(jnp.bfloat16)
            sent[2, :, lanes] = total_one
            sent[3, :, lanes] = grad_two
            copy = pltpu.make_async_copy(
                sent.at[:, :, lanes], kept.at[:, :, lanes], out_sems.at[group]
            )
            copy.start()
            outgoing.append(copy)

        section_back(
            made,
            lanes,
            functools.partial(loaded, group, 1),
            functools.partial(loaded, group, 0),
            store,
            keep,
        )
    for copy in outgoing:
        copy.wait()


def early_terms(width, *refs):
    kept = refs[: TICKS - 1]
    earlier, total, turn, fields, summed, sems, out_sems = refs[TICKS - 1 :]
    turn[...] = jnp.zeros_like(turn)
    edges = masks()
    copies = {}
    for group in range(width // GW):
        lanes = group_lanes(group)
        for tick in range(TICKS - 1):
            copies[group, tick] = pltpu.make_async_copy(
                kept[tick].at[:, :, lanes], fields.at[tick, :, :, lanes], sems.at[tick, group]
            )
            copies[group, tick].start()
    outgoing = []
    for group in range(width // GW):
        lanes = group_lanes(group)
        for tick in range(TICKS - 1):
            copies[group, tick].wait()
        for branch in range(2):
            columns = jnp.concatenate(
                [
                    column_shifts(fields[tick, branch, :, lanes].astype(jnp.float32), *edges)
                    for tick in range(TICKS - 1)
                ],
                axis=0,
            )
            rows = jnp.concatenate(
                [row_shifts(fields[tick, 2 + branch, :, lanes]) for tick in range(TICKS - 1)], axis=0
            )
            term = correlate(columns, rows)
            for a in range(3):
                summed[branch, pl.ds(a * 3 * GW, 3 * GW), lanes] = term[:, a * GW : (a + 1) * GW]
            copy = pltpu.make_async_copy(
                summed.at[branch, :, lanes], total.at[branch, :, lanes], out_sems.at[branch, group]
            )
            copy.start()
            outgoing.append(copy)
    for copy in outgoing:
        copy.wait()


def last_tick(half, width, places, received, top, kernels, total, earlier, *rest):
    made, final, mine, theirs, turn, held, summed, sent, sems, sem, total_sem, final_sem, share_sems = (
        rest[-13:]
    )
    loaded = kernel_loads(half, width, kernels, held, sems)
    total_copy = pltpu.make_async_copy(total, summed, total_sem)
    total_copy.start()
    turn[...] = jnp.zeros_like(turn)
    take_top(places, TICKS - 1, half, width, top, made, sem)
    outgoing = []
    for group in range(width // GW):
        lanes = group_lanes(group)

        def store(at, stream):
            made[at, :, lanes] = stream

        def keep(act_one, act_two, grad_two, total_one, columns_one, columns_two, rows_two, rows_one):
            if not group:
                total_copy.wait()
            for branch, pair in ((1, (columns_one, rows_two)), (0, (columns_two, rows_one))):
                term = correlate(*pair)
                for a in range(3):
                    rows = pl.ds(a * 3 * GW, 3 * GW)
                    sent[branch, rows, lanes] = (
                        summed[branch, rows, lanes] + term[:, a * GW : (a + 1) * GW]
                    ).astype(jnp.bfloat16)
                for slot in range(4):
                    for z_slot in range(2):
                        block = pl.multiple_of(places[1 + slot] + places[5 + z_slot], 16)
                        copy = pltpu.make_async_copy(
                            sent.at[branch, pl.ds(block, SHARE), lanes],
                            (mine, theirs)[slot // 2].at[slot % 2, z_slot, branch, :, lanes],
                            share_sems.at[branch, group, slot, z_slot],
                        )
                        copy.start()
                        outgoing.append(copy)

        section_back(
            made,
            lanes,
            functools.partial(loaded, group, 1),
            functools.partial(loaded, group, 0),
            store,
            keep,
        )
    copy = pltpu.make_async_copy(made, final.at[:, :, pl.ds(half * width, width)], final_sem)
    copy.start()
    outgoing.append(copy)
    for copy in outgoing:
        copy.wait()


ANY_REF = pl.BlockSpec(memory_space=pl.ANY)
VMEM_REF = pl.BlockSpec(memory_space=pltpu.VMEM)
SMEM_REF = pl.BlockSpec(memory_space=pltpu.SMEM)


def in_vmem(array):
    return pltpu.with_memory_space_constraint(array, pltpu.VMEM)


def in_hbm(array):
    return pltpu.with_memory_space_constraint(array, pltpu.HBM)


def params():
    return pltpu.CompilerParams(vmem_limit_bytes=VMEM_LIMIT)


def cost(products, width):
    groups = width // GW
    return pl.CostEstimate(
        flops=products * 2 * CELLS * ROWS * GW * groups,
        bytes_accessed=4 * 4 * CELLS * width,
        transcendentals=2 * CELLS * width,
    )


def passed_down(value):
    count = lax.axis_size("section")
    return lax.ppermute(value, "section", [(source, source - 1) for source in range(1, count)])


def partners(half, x):
    return (x ^ 1, 3 - x) if half == 0 else (3 - x, x ^ 1)


def share_places(half):
    x, z = lax.axis_index("dp_0"), lax.axis_index("dp_1")
    first, second = partners(half, x)
    is_top = lax.axis_index("section") == lax.axis_size("section") - 1
    blocks = [x, second, first, partners(half, first)[1]]
    rows = [block * (2 * SHARE) for block in blocks] + [z * SHARE, (1 - z) * SHARE]
    return jnp.stack([is_top.astype(jnp.int32)] + [row.astype(jnp.int32) for row in rows])


def first_sum(mine, came, earlier, passed, turn):
    turn[...] = jnp.zeros_like(turn)
    passed[...] = (mine[1].astype(jnp.float32) + came[1].astype(jnp.float32)).astype(jnp.bfloat16)


def second_sum(mine, came, came_next, earlier, across, kept, turn):
    turn[...] = jnp.zeros_like(turn)
    total = [
        mine[0, z_slot].astype(jnp.float32)
        + came[0, z_slot].astype(jnp.float32)
        + came_next[z_slot].astype(jnp.float32)
        for z_slot in range(2)
    ]
    kept[...] = total[0]
    across[...] = total[1].astype(jnp.bfloat16)


def last_sum(*refs):
    kept, came, out = refs[:HALVES], refs[HALVES:-1], refs[-1]
    for half in range(HALVES):
        width = kept[half].shape[-1]
        out[:, :, pl.ds(half * width, width)] = (
            kept[half][...] + came[half][...].astype(jnp.float32)
        ) * (1.0 / (HW * HW))


def summed_shares(mine, theirs, turn):
    width = mine[0].shape[-1]
    turn_type = pltpu.VMEM((8, 128), jnp.float32)
    halves = range(HALVES)
    pairs = [
        [[(x, partners(half, x)[step]) for x in range(4)] for step in range(2)] for half in halves
    ]
    came = [lax.ppermute(theirs[half], "dp_0", pairs[half][0]) for half in halves]
    came_next, came_last, kept = [], [], []
    for half in halves:
        passed, turn = pl.pallas_call(
            first_sum,
            out_shape=(pltpu.VMEM((2, 2, SHARE, width), jnp.bfloat16), turn_type),
            in_specs=[VMEM_REF, VMEM_REF, ANY_REF],
            out_specs=(VMEM_REF, VMEM_REF),
            compiler_params=params(),
            name=f"first_sum_{half}",
        )(mine[half], in_vmem(came[half]), turn)
        came_next.append(lax.ppermute(passed, "dp_0", pairs[half][1]))
    for half in halves:
        across, own, turn = pl.pallas_call(
            second_sum,
            out_shape=(
                pltpu.VMEM((2, SHARE, width), jnp.bfloat16),
                pltpu.VMEM((2, SHARE, width), jnp.float32),
                turn_type,
            ),
            in_specs=[VMEM_REF, VMEM_REF, VMEM_REF, ANY_REF],
            out_specs=(VMEM_REF, VMEM_REF, VMEM_REF),
            compiler_params=params(),
            name=f"second_sum_{half}",
        )(mine[half], in_vmem(came[half]), in_vmem(came_next[half]), turn)
        came_last.append(lax.ppermute(across, "dp_1", [(0, 1), (1, 0)]))
        kept.append(own)
    return pl.pallas_call(
        last_sum,
        out_shape=jax.ShapeDtypeStruct((2, SHARE, width * HALVES), jnp.float32),
        in_specs=[VMEM_REF] * (2 * HALVES),
        out_specs=VMEM_REF,
        compiler_params=params(),
        name="last_sum",
    )(*[in_vmem(own) for own in kept], *[in_vmem(part) for part in came_last])


def on_device(section_states, conv_kernels, top_feed):
    chans = section_states.shape[-1]
    width = chans // HALVES
    states = in_hbm(section_states.reshape(4, CELLS, chans))
    kernels = in_hbm(conv_kernels[0])
    top = in_hbm(top_feed.reshape(TICKS - 1, 4, CELLS, chans))
    places = [share_places(half) for half in range(HALVES)]

    groups = width // GW
    state_type = pltpu.VMEM((4, CELLS, width), jnp.bfloat16)
    kept_type = pltpu.HBM((4, CELLS, width), jnp.bfloat16)
    turn_type = pltpu.VMEM((8, 128), jnp.float32)
    held_scratch = pltpu.VMEM((2, ROWS, width), jnp.bfloat16)
    turn = jnp.zeros((8, 128), jnp.float32)
    made, kept = [None] * HALVES, [[] for _ in range(HALVES)]
    for tick in range(TICKS - 1):
        for half in range(HALVES):
            operands, specs = [states, kernels, turn], [ANY_REF] * 3
            if tick:
                operands = [places[half], in_vmem(made[half]), top, kernels, turn]
                specs = [SMEM_REF, VMEM_REF, ANY_REF, ANY_REF, ANY_REF]
            out, fields, turn = pl.pallas_call(
                functools.partial(early_tick, tick, half, width),
                out_shape=(state_type, kept_type, turn_type),
                in_specs=specs,
                out_specs=(VMEM_REF, ANY_REF, VMEM_REF),
                scratch_shapes=[
                    held_scratch,
                    pltpu.VMEM((4, CELLS, width), jnp.bfloat16),
                    pltpu.SemaphoreType.DMA((2, groups)),
                    pltpu.SemaphoreType.DMA((groups,)),
                    pltpu.SemaphoreType.DMA((groups,)),
                ],
                input_output_aliases={1: 0} if tick else {},
                compiler_params=params(),
                cost_estimate=cost(4, width),
                name=f"tick_{tick}_{half}",
            )(*operands)
            made[half] = passed_down(out)
            kept[half].append(in_hbm(fields))

    total = []
    for half in range(HALVES):
        summed, turn = pl.pallas_call(
            functools.partial(early_terms, width),
            out_shape=(pltpu.HBM((2, ROWS, width), jnp.float32), turn_type),
            in_specs=[ANY_REF] * TICKS,
            out_specs=(ANY_REF, VMEM_REF),
            scratch_shapes=[
                pltpu.VMEM((TICKS - 1, 4, CELLS, width), jnp.bfloat16),
                pltpu.VMEM((2, ROWS, width), jnp.float32),
                pltpu.SemaphoreType.DMA((TICKS - 1, groups)),
                pltpu.SemaphoreType.DMA((2, groups)),
            ],
            compiler_params=params(),
            cost_estimate=cost(2 * (TICKS - 1), width),
            name=f"early_terms_{half}",
        )(*kept[half], turn)
        total.append(in_hbm(summed))

    final = None
    mine, theirs = [None] * HALVES, [None] * HALVES
    share_type = pltpu.HBM((2, 2, 2, SHARE, width), jnp.bfloat16)
    for half in range(HALVES):
        operands = [places[half], in_vmem(made[half]), top, kernels, total[half], turn]
        specs = [SMEM_REF, VMEM_REF, ANY_REF, ANY_REF, ANY_REF, ANY_REF]
        aliases = {1: 0}
        if half:
            operands.append(in_hbm(final))
            specs.append(ANY_REF)
            aliases[6] = 1
        _, final, mine[half], theirs[half], turn = pl.pallas_call(
            functools.partial(last_tick, half, width),
            out_shape=(
                state_type,
                pltpu.HBM((4, CELLS, chans), jnp.bfloat16),
                share_type,
                share_type,
                turn_type,
            ),
            in_specs=specs,
            out_specs=(VMEM_REF, ANY_REF, ANY_REF, ANY_REF, VMEM_REF),
            scratch_shapes=[
                held_scratch,
                pltpu.VMEM((2, ROWS, width), jnp.float32),
                pltpu.VMEM((2, ROWS, width), jnp.bfloat16),
                pltpu.SemaphoreType.DMA((2, groups)),
                pltpu.SemaphoreType.DMA(()),
                pltpu.SemaphoreType.DMA(()),
                pltpu.SemaphoreType.DMA(()),
                pltpu.SemaphoreType.DMA((2, groups, 4, 2)),
            ],
            input_output_aliases=aliases,
            compiler_params=params(),
            cost_estimate=cost(6, width),
            name=f"last_tick_{half}",
        )(*operands)
    grads = summed_shares(mine, theirs, turn)
    return (final.reshape(1, 4, 1, HW, HW, chans), grads[None])


def solution(mesh):
    finer = Mesh(mesh.devices.reshape(mesh.shape["section"], 4, 2), ("section", "dp_0", "dp_1"))
    images = ("dp_0", "dp_1")
    in_specs = (
        P("section", None, images, None, None, None),
        P("section", None, None, None),
        P(None, None, images, None, None, None),
    )
    out_specs = (P("section", None, images, None, None, None), P("section", None, images, None))
    return jax.shard_map(
        on_device, mesh=finer, in_specs=in_specs, out_specs=out_specs, check_vma=False
    )
```

```python
import functools

import jax
import jax.numpy as jnp
from jax import lax
from jax.experimental import pallas as pl
from jax.experimental.pallas import tpu as pltpu
from jax.sharding import Mesh
from jax.sharding import PartitionSpec as P

GW = 128
HW = 16
TICKS = 4
CELLS = HW * HW
ROWS = 9 * GW
SHARE = ROWS // 8
HALVES = 2
FIRST = TICKS - 2
VMEM_LIMIT = 24 * 1024 * 1024


def column_shifts(field, at_left, at_right):
    before = jnp.where(at_left, 0.0, pltpu.roll(field, 1, 0))
    after = jnp.where(at_right, 0.0, pltpu.roll(field, CELLS - 1, 0))
    return jnp.concatenate(
        [before.astype(jnp.bfloat16), field.astype(jnp.bfloat16), after.astype(jnp.bfloat16)], axis=1
    )


def row_shifts(field):
    edge = jnp.zeros((HW, GW), field.dtype)
    up = jnp.concatenate([field[HW:], edge], axis=0)
    down = jnp.concatenate([edge, field[:-HW]], axis=0)
    return jnp.concatenate([up, field, down], axis=1)


def taps_by_row(kernel_ref, branch, lanes):
    return jnp.concatenate(
        [kernel_ref[branch, pl.ds(a * 3 * GW, 3 * GW), lanes] for a in range(3)], axis=1
    )


def conv(stack, kernel):
    parts = jnp.dot(stack, kernel, preferred_element_type=jnp.float32)
    edge = jnp.zeros((HW, GW), jnp.float32)
    above = jnp.concatenate([edge, parts[:-HW, :GW]], axis=0)
    below = jnp.concatenate([parts[HW:, 2 * GW :], edge], axis=0)
    return parts[:, GW : 2 * GW] + above + below


def conv_back(stack, kernel, at_left, at_right):
    parts = lax.dot_general(
        stack, kernel, (((1,), (1,)), ((), ())), preferred_element_type=jnp.float32
    )
    before = jnp.where(at_right, 0.0, pltpu.roll(parts[:, :GW], CELLS - 1, 0))
    after = jnp.where(at_left, 0.0, pltpu.roll(parts[:, 2 * GW :], 1, 0))
    return parts[:, GW : 2 * GW] + before + after


def correlate(columns, rows):
    return lax.dot_general(
        columns, rows, (((0,), (0,)), ((), ())), preferred_element_type=jnp.float32
    )


def masks():
    column = lax.rem(lax.broadcasted_iota(jnp.int32, (CELLS, GW), 0), HW)
    return column == 0, column == HW - 1


def masks():
    column = lax.rem(lax.broadcasted_iota(jnp.int32, (CELLS, GW), 0), HW)
    return column == 0, column == HW - 1


def group_lanes(group):
    return pl.ds(group * GW, GW)


def first_branch(state_ref, lanes, weights, keep):
    edges = masks()
    grad_two = state_ref[3, :, lanes]
    out_one = state_ref[0, :, lanes].astype(jnp.float32)
    sigma = jax.nn.sigmoid(out_one)
    slope = sigma * (1.0 + out_one * (1.0 - sigma))
    columns = column_shifts(out_one * sigma, *edges)
    rows = row_shifts(grad_two)
    keep(1, columns, rows)
    weights = weights()
    in_two = (state_ref[1, :, lanes].astype(jnp.float32) - conv(columns, weights)).astype(
        jnp.bfloat16
    )
    total_one = (
        state_ref[2, :, lanes].astype(jnp.float32) + conv_back(rows, weights, *edges) * slope
    ).astype(jnp.bfloat16)
    return in_two, total_one


def second_branch(state_ref, lanes, weights, in_two, total_one, keep):
    edges = masks()
    wide_two = in_two.astype(jnp.float32)
    sigma = jax.nn.sigmoid(wide_two)
    slope = sigma * (1.0 + wide_two * (1.0 - sigma))
    columns = column_shifts(wide_two * sigma, *edges)
    rows = row_shifts(total_one)
    keep(0, columns, rows)
    weights = weights()
    out_one = state_ref[0, :, lanes].astype(jnp.float32)
    grad_two = state_ref[3, :, lanes].astype(jnp.float32)
    state_ref[0, :, lanes] = (out_one - conv(columns, weights)).astype(jnp.bfloat16)
    state_ref[1, :, lanes] = in_two
    state_ref[2, :, lanes] = total_one
    state_ref[3, :, lanes] = (grad_two + conv_back(rows, weights, *edges) * slope).astype(
        jnp.bfloat16
    )


def section_back(state_ref, groups, weights, keep):
    halfway = [
        first_branch(
            state_ref,
            group_lanes(group),
            functools.partial(weights, group, 1),
            functools.partial(keep, group),
        )
        for group in range(groups)
    ]
    for group in range(groups):
        second_branch(
            state_ref,
            group_lanes(group),
            functools.partial(weights, group, 0),
            *halfway[group],
            functools.partial(keep, group),
        )


def take_state(places, tick, half, width, received, top, made, sem):
    @pl.when(places[0] == 1)
    def _():
        copy = pltpu.make_async_copy(
            top.at[tick - 1, :, :, pl.ds(half * width, width)], made, sem
        )
        copy.start()
        copy.wait()

    @pl.when(places[0] == 0)
    def _():
        made[...] = received[...]


def kernel_loads(half, width, kernels, held, sems):
    copies = {}
    for branch in (1, 0):
        for group in range(width // GW):
            wide = pl.ds(half * width + group * GW, GW)
            copies[group, branch] = pltpu.make_async_copy(
                kernels.at[branch, :, wide],
                held.at[branch, :, group_lanes(group)],
                sems.at[branch, group],
            )
            copies[group, branch].start()
    return copies


def early_tick(tick, half, width, *refs):
    groups = width // GW
    if (tick, half) == (0, 0):
        states, kernels, earlier, *refs = refs
    elif tick == 0:
        states, kernels, held, earlier, *refs = refs
    else:
        places, received, top, kernels, held, earlier, *refs = refs
    made, kept, turn, following, sent, next_sems, out_sems, *refs = refs
    loads = {}
    if tick == 0:
        state_sems, *refs = refs
        for group in range(groups):
            wide = pl.ds(half * width + group * GW, GW)
            loads[group] = pltpu.make_async_copy(
                states.at[:, :, wide], made.at[:, :, group_lanes(group)], state_sems.at[group]
            )
            loads[group].start()
    if (tick, half) == (0, 0):
        held, sems = refs
        loads.update(kernel_loads(half, width, kernels, held, sems))
    outgoing = list(
        kernel_loads((half + 1) % HALVES, width, kernels, following, next_sems).values()
    )
    turn[...] = jnp.zeros_like(turn)
    if tick:
        take_state(places, tick, half, width, received, top, made, refs[0])
    else:
        for group in range(groups):
            loads[group].wait()

    def weights(group, branch):
        if (group, branch) in loads:
            loads[group, branch].wait()
        return taps_by_row(held, branch, group_lanes(group))

    def keep(group, branch, columns, rows):
        lanes = group_lanes(group)
        sent[branch, 0, :, lanes] = columns[:, GW : 2 * GW]
        sent[branch, 1, :, lanes] = rows[:, GW : 2 * GW]
        if group == groups - 1:
            copy = pltpu.make_async_copy(sent.at[branch], kept.at[branch], out_sems.at[branch])
            copy.start()
            outgoing.append(copy)

    section_back(made, groups, weights, keep)
    for copy in outgoing:
        copy.wait()


def early_terms(width, *refs):
    kept = [refs[half * FIRST : (half + 1) * FIRST] for half in range(HALVES)]
    earlier, *refs = refs[HALVES * FIRST :]
    totals = refs[:HALVES]
    turn, fields, summed, sems, out_sems = refs[HALVES:]
    turn[...] = jnp.zeros_like(turn)
    edges = masks()
    copies = {}
    for half in range(HALVES):
        for tick in range(FIRST):
            copies[half, tick] = pltpu.make_async_copy(
                kept[half][tick], fields.at[half, tick], sems.at[half, tick]
            )
            copies[half, tick].start()
    outgoing = []
    for half in range(HALVES):
        for tick in range(FIRST):
            copies[half, tick].wait()
        for branch in range(2):
            for group in range(width // GW):
                lanes = group_lanes(group)
                planes = [
                    [fields[half, tick, branch, at, :, lanes] for tick in range(FIRST)]
                    for at in range(2)
                ]
                columns = [column_shifts(field.astype(jnp.float32), *edges) for field in planes[0]]
                rows = [row_shifts(field) for field in planes[1]]
                term = correlate(
                    jnp.concatenate(columns, axis=0), jnp.concatenate(rows, axis=0)
                ).astype(jnp.bfloat16)
                for a in range(3):
                    summed[half, branch, pl.ds(a * 3 * GW, 3 * GW), lanes] = term[
                        :, a * GW : (a + 1) * GW
                    ]
        copy = pltpu.make_async_copy(summed.at[half], totals[half], out_sems.at[half])
        copy.start()
        outgoing.append(copy)
    for copy in outgoing:
        copy.wait()


def last_tick(half, width, places, received, top, kernels, held, total, kept, earlier, *rest):
    if half:
        rest = rest[1:]
    made, final, mine, *rest = rest
    theirs, rest = rest[:2], rest[2:]
    groups = width // GW
    copies = []
    turn, *rest = rest
    if half + 1 < HALVES:
        following, summed, top_sem, final_sem, next_sems = rest
        copies.extend(kernel_loads(half + 1, width, kernels, following, next_sems).values())
    else:
        summed, top_sem, final_sem = rest
    turn[...] = jnp.zeros_like(turn)
    take_state(places, TICKS - 1, half, width, received, top, made, top_sem)
    stacks = {}

    def weights(group, branch):
        return taps_by_row(held, branch, group_lanes(group))

    def keep(group, branch, columns, rows):
        stacks[group, branch] = columns, rows

    section_back(made, groups, weights, keep)
    copy = pltpu.make_async_copy(made, final.at[:, :, pl.ds(half * width, width)], final_sem)
    copy.start()
    copies.append(copy)
    edges = masks()
    for branch in range(2):
        for group in range(groups):
            lanes = group_lanes(group)
            columns, rows = stacks[group, branch]
            early_columns = column_shifts(kept[branch, 0, :, lanes].astype(jnp.float32), *edges)
            term = correlate(
                jnp.concatenate([early_columns, columns], axis=0),
                jnp.concatenate([row_shifts(kept[branch, 1, :, lanes]), rows], axis=0),
            )
            for a in range(3):
                at = pl.ds(a * 3 * GW, 3 * GW)
                summed[branch, at, lanes] = (
                    total[branch, at, lanes].astype(jnp.float32) + term[:, a * GW : (a + 1) * GW]
                ).astype(jnp.bfloat16)
        for slot in range(4):
            for z_slot in range(2):
                block = pl.multiple_of(places[1 + 4 * branch + slot] + places[9 + z_slot], 16)
                share = summed[branch, pl.ds(block, SHARE), :]
                if slot < 2:
                    mine[branch, slot, z_slot] = share
                else:
                    theirs[branch][slot - 2, z_slot] = share
    for copy in copies:
        copy.wait()


ANY_REF = pl.BlockSpec(memory_space=pl.ANY)
VMEM_REF = pl.BlockSpec(memory_space=pltpu.VMEM)
SMEM_REF = pl.BlockSpec(memory_space=pltpu.SMEM)


def in_vmem(array):
    return pltpu.with_memory_space_constraint(array, pltpu.VMEM)


def in_hbm(array):
    return pltpu.with_memory_space_constraint(array, pltpu.HBM)


def params():
    return pltpu.CompilerParams(vmem_limit_bytes=VMEM_LIMIT)


def cost(products, width):
    groups = width // GW
    return pl.CostEstimate(
        flops=products * 2 * CELLS * ROWS * GW * groups,
        bytes_accessed=4 * 4 * CELLS * width,
        transcendentals=2 * CELLS * width,
    )


def passed_down(value):
    count = lax.axis_size("section")
    return lax.ppermute(value, "section", [(source, source - 1) for source in range(1, count)])


def partners(branch, x):
    return (x ^ 1, 3 - x) if branch == 0 else (3 - x, x ^ 1)


def share_places():
    x, z = lax.axis_index("dp_0"), lax.axis_index("dp_1")
    is_top = lax.axis_index("section") == lax.axis_size("section") - 1
    numbers = [is_top]
    for branch in range(2):
        first, second = partners(branch, x)
        numbers += [at * (2 * SHARE) for at in (x, second, first, partners(branch, first)[1])]
    numbers += [z * SHARE, (1 - z) * SHARE]
    return jnp.stack([number.astype(jnp.int32) for number in numbers])


def first_sum(mine, *refs):
    came, refs = refs[:2], refs[2:]
    earlier, passed, turn = refs[0], refs[1:3], refs[3]
    turn[...] = jnp.zeros_like(turn)
    for branch in range(2):
        passed[branch][...] = (
            mine[branch, 1].astype(jnp.float32) + came[branch][1].astype(jnp.float32)
        ).astype(jnp.bfloat16)


def second_sum(mine, *refs):
    came, came_next, refs = refs[:2], refs[2:4], refs[4:]
    earlier, across, kept, turn = refs
    turn[...] = jnp.zeros_like(turn)
    for branch in range(2):
        total = [
            mine[branch, 0, z_slot].astype(jnp.float32)
            + came[branch][0, z_slot].astype(jnp.float32)
            + came_next[branch][z_slot].astype(jnp.float32)
            for z_slot in range(2)
        ]
        kept[branch] = total[0]
        across[branch] = total[1].astype(jnp.bfloat16)


def last_sum(*refs):
    kept, came, out = refs[:HALVES], refs[HALVES:-1], refs[-1]
    for half in range(HALVES):
        width = kept[half].shape[-1]
        out[:, :, pl.ds(half * width, width)] = (
            kept[half][...] + came[half][...].astype(jnp.float32)
        ) * (1.0 / (HW * HW))


def summed_shares(mine, theirs, turn):
    width = mine[0].shape[-1]
    turn_type = pltpu.VMEM((8, 128), jnp.float32)
    halves = range(HALVES)
    pairs = [
        [[(x, partners(branch, x)[step]) for x in range(4)] for step in range(2)]
        for branch in range(2)
    ]
    passed_type = pltpu.VMEM((2, SHARE, width), jnp.bfloat16)
    came = [
        [in_vmem(lax.ppermute(theirs[half][b], "dp_0", pairs[b][0])) for b in range(2)]
        for half in halves
    ]
    came_next, came_last, kept = [], [], []
    for half in halves:
        *passed, turn = pl.pallas_call(
            first_sum,
            out_shape=(passed_type, passed_type, turn_type),
            in_specs=[VMEM_REF] * 3 + [ANY_REF],
            out_specs=(VMEM_REF,) * 3,
            compiler_params=params(),
            name=f"first_sum_{half}",
        )(mine[half], *came[half], turn)
        came_next.append(
            [in_vmem(lax.ppermute(passed[b], "dp_0", pairs[b][1])) for b in range(2)]
        )
    for half in halves:
        across, own, turn = pl.pallas_call(
            second_sum,
            out_shape=(passed_type, pltpu.VMEM((2, SHARE, width), jnp.float32), turn_type),
            in_specs=[VMEM_REF] * 5 + [ANY_REF],
            out_specs=(VMEM_REF, VMEM_REF, VMEM_REF),
            compiler_params=params(),
            name=f"second_sum_{half}",
        )(mine[half], *came[half], *came_next[half], turn)
        came_last.append(lax.ppermute(across, "dp_1", [(0, 1), (1, 0)]))
        kept.append(own)
    return pl.pallas_call(
        last_sum,
        out_shape=jax.ShapeDtypeStruct((2, SHARE, width * HALVES), jnp.float32),
        in_specs=[VMEM_REF] * (2 * HALVES),
        out_specs=VMEM_REF,
        compiler_params=params(),
        name="last_sum",
    )(*[in_vmem(own) for own in kept], *[in_vmem(part) for part in came_last])


def on_device(section_states, conv_kernels, top_feed):
    chans = section_states.shape[-1]
    width = chans // HALVES
    states = in_hbm(section_states.reshape(4, CELLS, chans))
    kernels = in_hbm(conv_kernels[0])
    top = in_hbm(top_feed.reshape(TICKS - 1, 4, CELLS, chans))
    places = share_places()

    groups = width // GW
    state_type = pltpu.VMEM((4, CELLS, width), jnp.bfloat16)
    kept_type = pltpu.HBM((2, 2, CELLS, width), jnp.bfloat16)
    held_type = pltpu.VMEM((2, ROWS, width), jnp.bfloat16)
    turn_type = pltpu.VMEM((8, 128), jnp.float32)
    dma = pltpu.SemaphoreType.DMA
    kept_scratch = pltpu.VMEM((2, 2, CELLS, width), jnp.bfloat16)
    turn = jnp.zeros((8, 128), jnp.float32)
    held = None
    made, kept = [None] * HALVES, [[] for _ in range(HALVES)]
    for tick in range(TICKS - 1):
        for half in range(HALVES):
            aliases = {}
            scratch = [kept_scratch, dma((2, groups)), dma((2,))]
            if tick:
                operands = [places, in_vmem(made[half]), top, kernels, held, turn]
                specs = [SMEM_REF, VMEM_REF, ANY_REF, ANY_REF, VMEM_REF, ANY_REF]
                aliases = {1: 0}
                scratch += [dma(())]
            elif half:
                operands, specs = [states, kernels, held, turn], [ANY_REF, ANY_REF, VMEM_REF, ANY_REF]
                scratch += [dma((groups,))]
            else:
                operands, specs = [states, kernels, turn], [ANY_REF] * 3
                scratch += [dma((groups,)), held_type, dma((2, groups))]
            out, fields, turn, following = pl.pallas_call(
                functools.partial(early_tick, tick, half, width),
                out_shape=(state_type, kept_type, turn_type, held_type),
                in_specs=specs,
                out_specs=(VMEM_REF, ANY_REF, VMEM_REF, VMEM_REF),
                scratch_shapes=scratch,
                input_output_aliases=aliases,
                compiler_params=params(),
                cost_estimate=cost(4, width),
                name=f"tick_{tick}_{half}",
            )(*operands)
            held = in_vmem(following)
            made[half] = passed_down(out)
            kept[half].append(fields)
            if (tick, half) == (FIRST, 0):
                *total, turn = pl.pallas_call(
                    functools.partial(early_terms, width),
                    out_shape=(
                        *[pltpu.HBM((2, ROWS, width), jnp.bfloat16) for _ in range(HALVES)],
                        turn_type,
                    ),
                    in_specs=[ANY_REF] * (HALVES * FIRST + 1),
                    out_specs=(*[ANY_REF] * HALVES, VMEM_REF),
                    scratch_shapes=[
                        pltpu.VMEM((HALVES, FIRST, 2, 2, CELLS, width), jnp.bfloat16),
                        pltpu.VMEM((HALVES, 2, ROWS, width), jnp.bfloat16),
                        dma((HALVES, FIRST)),
                        dma((HALVES,)),
                    ],
                    compiler_params=params(),
                    cost_estimate=cost(2 * FIRST * HALVES, width),
                    name="early_terms",
                )(*[in_hbm(plane) for side in kept for plane in side[:FIRST]], turn)

    final = None
    mine, theirs = [None] * HALVES, [None] * HALVES
    theirs_type = pltpu.VMEM((2, 2, SHARE, width), jnp.bfloat16)
    for half in range(HALVES):
        operands = [places, in_vmem(made[half]), top, kernels, held, total[half], kept[half][FIRST], turn]
        specs = [SMEM_REF, VMEM_REF, ANY_REF, ANY_REF, VMEM_REF, VMEM_REF, VMEM_REF, ANY_REF]
        aliases = {1: 0}
        if half:
            aliases[len(operands)] = 1
            operands.append(in_hbm(final))
            specs.append(ANY_REF)
        more = half + 1 < HALVES
        _, final, mine[half], *theirs[half], turn = pl.pallas_call(
            functools.partial(last_tick, half, width),
            out_shape=(
                state_type,
                pltpu.HBM((4, CELLS, chans), jnp.bfloat16),
                pltpu.VMEM((2, 2, 2, SHARE, width), jnp.bfloat16),
                theirs_type,
                theirs_type,
                turn_type,
                *[held_type] * more,
            ),
            in_specs=specs,
            out_specs=(VMEM_REF, ANY_REF, *[VMEM_REF] * (4 + more)),
            scratch_shapes=[
                pltpu.VMEM((2, ROWS, width), jnp.bfloat16),
                dma(()),
                dma(()),
                *[dma((2, groups))] * more,
            ],
            input_output_aliases=aliases,
            compiler_params=params(),
            cost_estimate=cost(6, width),
            name=f"last_tick_{half}",
        )(*operands)
        if more:
            held = in_vmem(turn)
            *theirs[half], turn = theirs[half]
    grads = summed_shares(mine, theirs, turn)
    return (final.reshape(1, 4, 1, HW, HW, chans), grads[None])


def solution(mesh):
    finer = Mesh(mesh.devices.reshape(mesh.shape["section"], 4, 2), ("section", "dp_0", "dp_1"))
    images = ("dp_0", "dp_1")
    in_specs = (
        P("section", None, images, None, None, None),
        P("section", None, None, None),
        P(None, None, images, None, None, None),
    )
    out_specs = (P("section", None, images, None, None, None), P("section", None, images, None))
    return jax.shard_map(
        on_device, mesh=finer, in_specs=in_specs, out_specs=out_specs, check_vma=False
    )
```

```python
import functools

import jax
import jax.numpy as jnp
from jax import lax
from jax.experimental import pallas as pl
from jax.experimental.pallas import tpu as pltpu
from jax.sharding import Mesh
from jax.sharding import PartitionSpec as P

GW = 128
HW = 16
TICKS = 4
CELLS = HW * HW
ROWS = 9 * GW
SHARE = ROWS // 8
HALVES = 2
FIRST = TICKS - 2
VMEM_LIMIT = 24 * 1024 * 1024


def column_shifts(field, at_left, at_right):
    before = jnp.where(at_left, 0.0, pltpu.roll(field, 1, 0))
    after = jnp.where(at_right, 0.0, pltpu.roll(field, CELLS - 1, 0))
    return jnp.concatenate(
        [before.astype(jnp.bfloat16), field.astype(jnp.bfloat16), after.astype(jnp.bfloat16)], axis=1
    )


def row_shifts(field):
    edge = jnp.zeros((HW, GW), field.dtype)
    up = jnp.concatenate([field[HW:], edge], axis=0)
    down = jnp.concatenate([edge, field[:-HW]], axis=0)
    return jnp.concatenate([up, field, down], axis=1)


def taps_by_row(kernel_ref, branch, lanes):
    return jnp.concatenate(
        [kernel_ref[branch, pl.ds(a * 3 * GW, 3 * GW), lanes] for a in range(3)], axis=1
    )


def conv(stack, kernel):
    parts = jnp.dot(stack, kernel, preferred_element_type=jnp.float32)
    edge = jnp.zeros((HW, GW), jnp.float32)
    above = jnp.concatenate([edge, parts[:-HW, :GW]], axis=0)
    below = jnp.concatenate([parts[HW:, 2 * GW :], edge], axis=0)
    return parts[:, GW : 2 * GW] + above + below


def conv_back(stack, kernel, at_left, at_right):
    parts = lax.dot_general(
        stack, kernel, (((1,), (1,)), ((), ())), preferred_element_type=jnp.float32
    )
    before = jnp.where(at_right, 0.0, pltpu.roll(parts[:, :GW], CELLS - 1, 0))
    after = jnp.where(at_left, 0.0, pltpu.roll(parts[:, 2 * GW :], 1, 0))
    return parts[:, GW : 2 * GW] + before + after


def correlate(columns, rows):
    return lax.dot_general(
        columns, rows, (((0,), (0,)), ((), ())), preferred_element_type=jnp.float32
    )


def masks():
    column = lax.rem(lax.broadcasted_iota(jnp.int32, (CELLS, GW), 0), HW)
    return column == 0, column == HW - 1


def masks():
    column = lax.rem(lax.broadcasted_iota(jnp.int32, (CELLS, GW), 0), HW)
    return column == 0, column == HW - 1


def group_lanes(group):
    return pl.ds(group * GW, GW)


def first_branch(state_ref, lanes, weights, keep):
    edges = masks()
    grad_two = state_ref[3, :, lanes]
    out_one = state_ref[0, :, lanes].astype(jnp.float32)
    sigma = jax.nn.sigmoid(out_one)
    slope = sigma * (1.0 + out_one * (1.0 - sigma))
    columns = column_shifts(out_one * sigma, *edges)
    rows = row_shifts(grad_two)
    keep(1, columns, rows)
    weights = weights()
    in_two = (state_ref[1, :, lanes].astype(jnp.float32) - conv(columns, weights)).astype(
        jnp.bfloat16
    )
    total_one = (
        state_ref[2, :, lanes].astype(jnp.float32) + conv_back(rows, weights, *edges) * slope
    ).astype(jnp.bfloat16)
    return in_two, total_one


def second_branch(state_ref, lanes, weights, in_two, total_one, keep):
    edges = masks()
    wide_two = in_two.astype(jnp.float32)
    sigma = jax.nn.sigmoid(wide_two)
    slope = sigma * (1.0 + wide_two * (1.0 - sigma))
    columns = column_shifts(wide_two * sigma, *edges)
    rows = row_shifts(total_one)
    keep(0, columns, rows)
    weights = weights()
    out_one = state_ref[0, :, lanes].astype(jnp.float32)
    grad_two = state_ref[3, :, lanes].astype(jnp.float32)
    state_ref[0, :, lanes] = (out_one - conv(columns, weights)).astype(jnp.bfloat16)
    state_ref[1, :, lanes] = in_two
    state_ref[2, :, lanes] = total_one
    state_ref[3, :, lanes] = (grad_two + conv_back(rows, weights, *edges) * slope).astype(
        jnp.bfloat16
    )


def section_back(state_ref, groups, weights, keep):
    halfway = [
        first_branch(
            state_ref,
            group_lanes(group),
            functools.partial(weights, group, 1),
            functools.partial(keep, group),
        )
        for group in range(groups)
    ]
    for group in range(groups):
        second_branch(
            state_ref,
            group_lanes(group),
            functools.partial(weights, group, 0),
            *halfway[group],
            functools.partial(keep, group),
        )


def take_state(tick, half, width, received, top, made, sem):
    is_top = lax.axis_index("section") == lax.axis_size("section") - 1

    @pl.when(is_top)
    def _():
        copy = pltpu.make_async_copy(
            top.at[tick - 1, :, :, pl.ds(half * width, width)], made, sem
        )
        copy.start()
        copy.wait()

    @pl.when(jnp.logical_not(is_top))
    def _():
        made[...] = received[...]


def started(*copies):
    for copy in copies:
        copy.start()
    return list(copies)


def early_tick(tick, half, width, *refs):
    groups = width // GW
    made, kept, turn, following = None, None, None, None
    loads, outgoing = {}, []
    if tick == 0:
        if half == 0:
            states, kernels, earlier, made, kept, turn, following, stored, *refs = refs
            sent, next_sems, out_sems, state_sem, stored_sems, held, sems = refs
        else:
            states, kernels, held, store_next, earlier, made, kept, turn, following, stored, *refs = refs
            sent, next_sems, out_sems, state_sem, stored_sems = refs
        wide = pl.ds(half * width, width)
        (state_load,) = started(pltpu.make_async_copy(states.at[:, :, wide], made, state_sem))
        if half == 0:
            for branch in (1, 0):
                (loads[branch],) = started(
                    pltpu.make_async_copy(
                        kernels.at[branch, :, wide], held.at[branch], sems.at[branch]
                    )
                )
            later = pl.ds(width, width)
            sources = [kernels.at[branch, :, later] for branch in range(2)]
        else:
            sources = [store_next.at[branch] for branch in range(2)]
            for branch in (1, 0):
                outgoing += started(
                    pltpu.make_async_copy(held.at[branch], stored.at[branch], stored_sems.at[branch])
                )
    else:
        received, top, store_next, held, earlier, made, kept, turn, following, *refs = refs
        sent, next_sems, out_sems, top_sem = refs
        sources = [store_next.at[branch] for branch in range(2)]
    for branch in (1, 0):
        outgoing += started(
            pltpu.make_async_copy(sources[branch], following.at[branch], next_sems.at[branch])
        )
    turn[...] = jnp.zeros_like(turn)
    if tick:
        take_state(tick, half, width, received, top, made, top_sem)
    else:
        state_load.wait()

    def weights(group, branch):
        if group == 0 and branch in loads:
            loads[branch].wait()
            outgoing.extend(
                started(
                    pltpu.make_async_copy(held.at[branch], stored.at[branch], stored_sems.at[branch])
                )
            )
        return taps_by_row(held, branch, group_lanes(group))

    def keep(group, branch, columns, rows):
        lanes = group_lanes(group)
        sent[branch, 0, :, lanes] = columns[:, GW : 2 * GW]
        sent[branch, 1, :, lanes] = rows[:, GW : 2 * GW]
        if group == groups - 1:
            outgoing.extend(
                started(pltpu.make_async_copy(sent.at[branch], kept.at[branch], out_sems.at[branch]))
            )

    section_back(made, groups, weights, keep)
    for copy in outgoing:
        copy.wait()


def early_terms(width, *refs):
    kept = [refs[half * FIRST : (half + 1) * FIRST] for half in range(HALVES)]
    earlier, *refs = refs[HALVES * FIRST :]
    totals = refs[:HALVES]
    turn, fields, summed, sems, out_sems = refs[HALVES:]
    turn[...] = jnp.zeros_like(turn)
    edges = masks()
    copies = {}
    for half in range(HALVES):
        for tick in range(FIRST):
            copies[half, tick] = pltpu.make_async_copy(
                kept[half][tick], fields.at[half, tick], sems.at[half, tick]
            )
            copies[half, tick].start()
    outgoing = []
    for half in range(HALVES):
        for tick in range(FIRST):
            copies[half, tick].wait()
        for branch in range(2):
            for group in range(width // GW):
                lanes = group_lanes(group)
                planes = [
                    [fields[half, tick, branch, at, :, lanes] for tick in range(FIRST)]
                    for at in range(2)
                ]
                columns = [column_shifts(field.astype(jnp.float32), *edges) for field in planes[0]]
                rows = [row_shifts(field) for field in planes[1]]
                term = correlate(
                    jnp.concatenate(columns, axis=0), jnp.concatenate(rows, axis=0)
                ).astype(jnp.bfloat16)
                for a in range(3):
                    summed[half, branch, pl.ds(a * 3 * GW, 3 * GW), lanes] = term[
                        :, a * GW : (a + 1) * GW
                    ]
        copy = pltpu.make_async_copy(summed.at[half], totals[half], out_sems.at[half])
        copy.start()
        outgoing.append(copy)
    for copy in outgoing:
        copy.wait()


def last_tick(half, width, received, top, store_next, held, total, kept, earlier, *rest):
    if half:
        rest = rest[1:]
    made, final, mine, *rest = rest
    theirs, rest = rest[:2], rest[2:]
    groups = width // GW
    copies = []
    turn, *rest = rest
    if half + 1 < HALVES:
        following, summed, top_sem, final_sem, next_sems = rest
        for branch in (1, 0):
            copies += started(
                pltpu.make_async_copy(
                    store_next.at[branch], following.at[branch], next_sems.at[branch]
                )
            )
    else:
        summed, top_sem, final_sem = rest
    turn[...] = jnp.zeros_like(turn)
    take_state(TICKS - 1, half, width, received, top, made, top_sem)
    stacks = {}

    def weights(group, branch):
        return taps_by_row(held, branch, group_lanes(group))

    def keep(group, branch, columns, rows):
        stacks[group, branch] = columns, rows

    section_back(made, groups, weights, keep)
    copy = pltpu.make_async_copy(made, final.at[:, :, pl.ds(half * width, width)], final_sem)
    copy.start()
    copies.append(copy)
    edges = masks()
    z = lax.axis_index("dp_1")
    for branch in range(2):
        for group in range(groups):
            lanes = group_lanes(group)
            columns, rows = stacks[group, branch]
            early_columns = column_shifts(kept[branch, 0, :, lanes].astype(jnp.float32), *edges)
            term = correlate(
                jnp.concatenate([early_columns, columns], axis=0),
                jnp.concatenate([row_shifts(kept[branch, 1, :, lanes]), rows], axis=0),
            )
            for a in range(3):
                at = pl.ds(a * 3 * GW, 3 * GW)
                summed[branch, at, lanes] = (
                    total[branch, at, lanes].astype(jnp.float32) + term[:, a * GW : (a + 1) * GW]
                ).astype(jnp.bfloat16)
        for slot, block in enumerate(share_blocks(branch)):
            for z_slot in range(2):
                first = pl.multiple_of((2 * block + (z ^ z_slot)) * SHARE, 16)
                share = summed[branch, pl.ds(first, SHARE), :]
                if slot < 2:
                    mine[branch, slot, z_slot] = share
                else:
                    theirs[branch][slot - 2, z_slot] = share
    for copy in copies:
        copy.wait()


ANY_REF = pl.BlockSpec(memory_space=pl.ANY)
VMEM_REF = pl.BlockSpec(memory_space=pltpu.VMEM)


def in_vmem(array):
    return pltpu.with_memory_space_constraint(array, pltpu.VMEM)


def in_hbm(array):
    return pltpu.with_memory_space_constraint(array, pltpu.HBM)


def params():
    return pltpu.CompilerParams(vmem_limit_bytes=VMEM_LIMIT)


def cost(products, width):
    groups = width // GW
    return pl.CostEstimate(
        flops=products * 2 * CELLS * ROWS * GW * groups,
        bytes_accessed=4 * 4 * CELLS * width,
        transcendentals=2 * CELLS * width,
    )


def passed_down(value):
    count = lax.axis_size("section")
    return lax.ppermute(value, "section", [(source, source - 1) for source in range(1, count)])


def partners(branch, x):
    return (x ^ 1, 3 - x) if branch == 0 else (3 - x, x ^ 1)


def share_blocks(branch):
    x = lax.axis_index("dp_0")
    first, second = partners(branch, x)
    return x, second, first, partners(branch, first)[1]


def first_sum(mine, *refs):
    came, refs = refs[:2], refs[2:]
    earlier, passed, turn = refs[0], refs[1:3], refs[3]
    turn[...] = jnp.zeros_like(turn)
    for branch in range(2):
        passed[branch][...] = (
            mine[branch, 1].astype(jnp.float32) + came[branch][1].astype(jnp.float32)
        ).astype(jnp.bfloat16)


def second_sum(mine, *refs):
    came, came_next, refs = refs[:2], refs[2:4], refs[4:]
    earlier, across, kept, turn = refs
    turn[...] = jnp.zeros_like(turn)
    for branch in range(2):
        total = [
            mine[branch, 0, z_slot].astype(jnp.float32)
            + came[branch][0, z_slot].astype(jnp.float32)
            + came_next[branch][z_slot].astype(jnp.float32)
            for z_slot in range(2)
        ]
        kept[branch] = total[0]
        across[branch] = total[1].astype(jnp.bfloat16)


def last_sum(*refs):
    kept, came, out = refs[:HALVES], refs[HALVES:-1], refs[-1]
    for half in range(HALVES):
        width = kept[half].shape[-1]
        out[:, :, pl.ds(half * width, width)] = (
            kept[half][...] + came[half][...].astype(jnp.float32)
        ) * (1.0 / (HW * HW))


def summed_shares(mine, theirs, turn):
    width = mine[0].shape[-1]
    turn_type = pltpu.VMEM((8, 128), jnp.float32)
    halves = range(HALVES)
    pairs = [
        [[(x, partners(branch, x)[step]) for x in range(4)] for step in range(2)]
        for branch in range(2)
    ]
    passed_type = pltpu.VMEM((2, SHARE, width), jnp.bfloat16)
    came = [
        [in_vmem(lax.ppermute(theirs[half][b], "dp_0", pairs[b][0])) for b in range(2)]
        for half in halves
    ]
    came_next, came_last, kept = [], [], []
    for half in halves:
        *passed, turn = pl.pallas_call(
            first_sum,
            out_shape=(passed_type, passed_type, turn_type),
            in_specs=[VMEM_REF] * 3 + [ANY_REF],
            out_specs=(VMEM_REF,) * 3,
            compiler_params=params(),
            name=f"first_sum_{half}",
        )(mine[half], *came[half], turn)
        came_next.append(
            [in_vmem(lax.ppermute(passed[b], "dp_0", pairs[b][1])) for b in range(2)]
        )
    for half in halves:
        across, own, turn = pl.pallas_call(
            second_sum,
            out_shape=(passed_type, pltpu.VMEM((2, SHARE, width), jnp.float32), turn_type),
            in_specs=[VMEM_REF] * 5 + [ANY_REF],
            out_specs=(VMEM_REF, VMEM_REF, VMEM_REF),
            compiler_params=params(),
            name=f"second_sum_{half}",
        )(mine[half], *came[half], *came_next[half], turn)
        came_last.append(lax.ppermute(across, "dp_1", [(0, 1), (1, 0)]))
        kept.append(own)
    return pl.pallas_call(
        last_sum,
        out_shape=jax.ShapeDtypeStruct((2, SHARE, width * HALVES), jnp.float32),
        in_specs=[VMEM_REF] * (2 * HALVES),
        out_specs=VMEM_REF,
        compiler_params=params(),
        name="last_sum",
    )(*[in_vmem(own) for own in kept], *[in_vmem(part) for part in came_last])


def on_device(section_states, conv_kernels, top_feed):
    chans = section_states.shape[-1]
    width = chans // HALVES
    states = in_hbm(section_states.reshape(4, CELLS, chans))
    kernels = in_hbm(conv_kernels[0])
    top = in_hbm(top_feed.reshape(TICKS - 1, 4, CELLS, chans))

    groups = width // GW
    state_type = pltpu.VMEM((4, CELLS, width), jnp.bfloat16)
    kept_type = pltpu.HBM((2, 2, CELLS, width), jnp.bfloat16)
    held_type = pltpu.VMEM((2, ROWS, width), jnp.bfloat16)
    turn_type = pltpu.VMEM((8, 128), jnp.float32)
    dma = pltpu.SemaphoreType.DMA
    kept_scratch = pltpu.VMEM((2, 2, CELLS, width), jnp.bfloat16)
    turn = jnp.zeros((8, 128), jnp.float32)
    held, stored = None, []
    stored_type = pltpu.HBM((2, ROWS, width), jnp.bfloat16)
    made, kept = [None] * HALVES, [[] for _ in range(HALVES)]
    for tick in range(TICKS - 1):
        for half in range(HALVES):
            if (tick, half) == (FIRST, 0):
                *total, turn = pl.pallas_call(
                    functools.partial(early_terms, width),
                    out_shape=(
                        *[pltpu.HBM((2, ROWS, width), jnp.bfloat16) for _ in range(HALVES)],
                        turn_type,
                    ),
                    in_specs=[ANY_REF] * (HALVES * FIRST + 1),
                    out_specs=(*[ANY_REF] * HALVES, VMEM_REF),
                    scratch_shapes=[
                        pltpu.VMEM((HALVES, FIRST, 2, 2, CELLS, width), jnp.bfloat16),
                        pltpu.VMEM((HALVES, 2, ROWS, width), jnp.bfloat16),
                        dma((HALVES, FIRST)),
                        dma((HALVES,)),
                    ],
                    compiler_params=params(),
                    cost_estimate=cost(2 * FIRST * HALVES, width),
                    name="early_terms",
                )(*[in_hbm(plane) for side in kept for plane in side], turn)
            aliases = {}
            outs = [state_type, kept_type, turn_type, held_type]
            out_specs = [VMEM_REF, ANY_REF, VMEM_REF, VMEM_REF]
            scratch = [kept_scratch, dma((2,)), dma((2,)), dma(())]
            if tick:
                operands = [in_vmem(made[half]), top, stored[1 - half], held, turn]
                specs = [VMEM_REF, ANY_REF, ANY_REF, VMEM_REF, ANY_REF]
                aliases = {0: 0}
            else:
                outs.append(stored_type)
                out_specs.append(ANY_REF)
                scratch.append(dma((2,)))
                if half:
                    operands = [states, kernels, held, stored[0], turn]
                    specs = [ANY_REF, ANY_REF, VMEM_REF, ANY_REF, ANY_REF]
                else:
                    operands, specs = [states, kernels, turn], [ANY_REF] * 3
                    scratch += [held_type, dma((2,))]
            out, fields, turn, following, *rest = pl.pallas_call(
                functools.partial(early_tick, tick, half, width),
                out_shape=tuple(outs),
                in_specs=specs,
                out_specs=tuple(out_specs),
                scratch_shapes=scratch,
                input_output_aliases=aliases,
                compiler_params=params(),
                cost_estimate=cost(4, width),
                name=f"tick_{tick}_{half}",
            )(*operands)
            stored += [in_hbm(copy) for copy in rest]
            held = in_vmem(following)
            made[half] = passed_down(out)
            kept[half].append(fields)

    final = None
    mine, theirs = [None] * HALVES, [None] * HALVES
    theirs_type = pltpu.VMEM((2, 2, SHARE, width), jnp.bfloat16)
    for half in range(HALVES):
        operands = [in_vmem(made[half]), top, stored[1], held, total[half], kept[half][FIRST], turn]
        specs = [VMEM_REF, ANY_REF, ANY_REF, VMEM_REF, VMEM_REF, VMEM_REF, ANY_REF]
        aliases = {0: 0}
        if half:
            aliases[len(operands)] = 1
            operands.append(in_hbm(final))
            specs.append(ANY_REF)
        more = half + 1 < HALVES
        _, final, mine[half], *theirs[half], turn = pl.pallas_call(
            functools.partial(last_tick, half, width),
            out_shape=(
                state_type,
                pltpu.HBM((4, CELLS, chans), jnp.bfloat16),
                pltpu.VMEM((2, 2, 2, SHARE, width), jnp.bfloat16),
                theirs_type,
                theirs_type,
                turn_type,
                *[held_type] * more,
            ),
            in_specs=specs,
            out_specs=(VMEM_REF, ANY_REF, *[VMEM_REF] * (4 + more)),
            scratch_shapes=[
                pltpu.VMEM((2, ROWS, width), jnp.bfloat16),
                dma(()),
                dma(()),
                *[dma((2,))] * more,
            ],
            input_output_aliases=aliases,
            compiler_params=params(),
            cost_estimate=cost(6, width),
            name=f"last_tick_{half}",
        )(*operands)
        if more:
            held = in_vmem(turn)
            *theirs[half], turn = theirs[half]
    grads = summed_shares(mine, theirs, turn)
    return (final.reshape(1, 4, 1, HW, HW, chans), grads[None])


def solution(mesh):
    finer = Mesh(mesh.devices.reshape(mesh.shape["section"], 4, 2), ("section", "dp_0", "dp_1"))
    images = ("dp_0", "dp_1")
    in_specs = (
        P("section", None, images, None, None, None),
        P("section", None, None, None),
        P(None, None, images, None, None, None),
    )
    out_specs = (P("section", None, images, None, None, None), P("section", None, images, None))
    return jax.shard_map(
        on_device, mesh=finer, in_specs=in_specs, out_specs=out_specs, check_vma=False
    )
```

```python
import functools

import jax
import jax.numpy as jnp
from jax import lax
from jax.experimental import pallas as pl
from jax.experimental.pallas import tpu as pltpu
from jax.sharding import Mesh
from jax.sharding import PartitionSpec as P

GW = 128
HW = 16
TICKS = 4
CELLS = HW * HW
ROWS = 9 * GW
SHARE = ROWS // 8
HALVES = 2
FIRST = TICKS - 2
VMEM_LIMIT = 24 * 1024 * 1024


def column_shifts(field, at_left, at_right):
    before = jnp.where(at_left, 0.0, pltpu.roll(field, 1, 0))
    after = jnp.where(at_right, 0.0, pltpu.roll(field, CELLS - 1, 0))
    return jnp.concatenate(
        [before.astype(jnp.bfloat16), field.astype(jnp.bfloat16), after.astype(jnp.bfloat16)], axis=1
    )


def row_shifts(field):
    edge = jnp.zeros((HW, GW), field.dtype)
    up = jnp.concatenate([field[HW:], edge], axis=0)
    down = jnp.concatenate([edge, field[:-HW]], axis=0)
    return jnp.concatenate([up, field, down], axis=1)


def taps_by_row(kernel_ref, branch, lanes):
    return jnp.concatenate(
        [kernel_ref[branch, pl.ds(a * 3 * GW, 3 * GW), lanes] for a in range(3)], axis=1
    )


def conv(stack, kernel):
    parts = jnp.dot(stack, kernel, preferred_element_type=jnp.float32)
    edge = jnp.zeros((HW, GW), jnp.float32)
    above = jnp.concatenate([edge, parts[:-HW, :GW]], axis=0)
    below = jnp.concatenate([parts[HW:, 2 * GW :], edge], axis=0)
    return parts[:, GW : 2 * GW] + above + below


def conv_back(stack, kernel, at_left, at_right):
    parts = lax.dot_general(
        stack, kernel, (((1,), (1,)), ((), ())), preferred_element_type=jnp.float32
    )
    before = jnp.where(at_right, 0.0, pltpu.roll(parts[:, :GW], CELLS - 1, 0))
    after = jnp.where(at_left, 0.0, pltpu.roll(parts[:, 2 * GW :], 1, 0))
    return parts[:, GW : 2 * GW] + before + after


def correlate(columns, rows):
    return lax.dot_general(
        columns, rows, (((0,), (0,)), ((), ())), preferred_element_type=jnp.float32
    )


def masks():
    column = lax.rem(lax.broadcasted_iota(jnp.int32, (CELLS, GW), 0), HW)
    return column == 0, column == HW - 1


def masks():
    column = lax.rem(lax.broadcasted_iota(jnp.int32, (CELLS, GW), 0), HW)
    return column == 0, column == HW - 1


def group_lanes(group):
    return pl.ds(group * GW, GW)


def first_branch(state_ref, lanes, weights, keep):
    edges = masks()
    grad_two = state_ref[3, :, lanes]
    out_one = state_ref[0, :, lanes].astype(jnp.float32)
    sigma = jax.nn.sigmoid(out_one)
    slope = sigma * (1.0 + out_one * (1.0 - sigma))
    columns = column_shifts(out_one * sigma, *edges)
    rows = row_shifts(grad_two)
    keep(1, columns, rows)
    weights = weights()
    in_two = (state_ref[1, :, lanes].astype(jnp.float32) - conv(columns, weights)).astype(
        jnp.bfloat16
    )
    total_one = (
        state_ref[2, :, lanes].astype(jnp.float32) + conv_back(rows, weights, *edges) * slope
    ).astype(jnp.bfloat16)
    return in_two, total_one


def second_branch(state_ref, lanes, weights, in_two, total_one, keep):
    edges = masks()
    wide_two = in_two.astype(jnp.float32)
    sigma = jax.nn.sigmoid(wide_two)
    slope = sigma * (1.0 + wide_two * (1.0 - sigma))
    columns = column_shifts(wide_two * sigma, *edges)
    rows = row_shifts(total_one)
    keep(0, columns, rows)
    weights = weights()
    out_one = state_ref[0, :, lanes].astype(jnp.float32)
    grad_two = state_ref[3, :, lanes].astype(jnp.float32)
    state_ref[0, :, lanes] = (out_one - conv(columns, weights)).astype(jnp.bfloat16)
    state_ref[1, :, lanes] = in_two
    state_ref[2, :, lanes] = total_one
    state_ref[3, :, lanes] = (grad_two + conv_back(rows, weights, *edges) * slope).astype(
        jnp.bfloat16
    )


def section_back(state_ref, groups, weights, keep):
    halfway = [
        first_branch(
            state_ref,
            group_lanes(group),
            functools.partial(weights, group, 1),
            functools.partial(keep, group),
        )
        for group in range(groups)
    ]
    for group in range(groups):
        second_branch(
            state_ref,
            group_lanes(group),
            functools.partial(weights, group, 0),
            *halfway[group],
            functools.partial(keep, group),
        )


def take_state(tick, half, width, received, top, made, sem):
    is_top = lax.axis_index("section") == lax.axis_size("section") - 1

    @pl.when(is_top)
    def _():
        copy = pltpu.make_async_copy(
            top.at[tick - 1, :, :, pl.ds(half * width, width)], made, sem
        )
        copy.start()
        copy.wait()

    @pl.when(jnp.logical_not(is_top))
    def _():
        made[...] = received[...]


def started(*copies):
    for copy in copies:
        copy.start()
    return list(copies)


def kernel_copies(half, width, kernels, held, sems):
    wide = pl.ds(half * width, width)
    return [
        pltpu.make_async_copy(kernels.at[branch, :, wide], held.at[branch], sems.at[branch])
        for branch in range(2)
    ]


def early_tick(tick, half, width, *refs):
    groups = width // GW
    loads, outgoing = [], []
    if tick == 0:
        states, kernels, *refs = refs
        if half:
            held, *refs = refs
        earlier, made, kept, turn, following, sent, out_sems, state_sem, next_sems, *refs = refs
        (state_load,) = started(
            pltpu.make_async_copy(states.at[:, :, pl.ds(half * width, width)], made, state_sem)
        )
        if not half:
            held, sems = refs
            loads = kernel_copies(half, width, kernels, held, sems)
            started(*loads[::-1])
    else:
        received, top, kernels, held, earlier, made, kept, turn, following, *refs = refs
        sent, out_sems, top_sem, next_sems = refs
    outgoing += started(
        *kernel_copies((half + 1) % HALVES, width, kernels, following, next_sems)[::-1]
    )
    turn[...] = jnp.zeros_like(turn)
    if tick:
        take_state(tick, half, width, received, top, made, top_sem)
    else:
        state_load.wait()

    def weights(group, branch):
        if group == 0 and loads:
            loads[branch].wait()
        return taps_by_row(held, branch, group_lanes(group))

    def keep(group, branch, columns, rows):
        lanes = group_lanes(group)
        sent[branch, 0, :, lanes] = columns[:, GW : 2 * GW]
        sent[branch, 1, :, lanes] = rows[:, GW : 2 * GW]
        if group == groups - 1:
            outgoing.extend(
                started(pltpu.make_async_copy(sent.at[branch], kept.at[branch], out_sems.at[branch]))
            )

    section_back(made, groups, weights, keep)
    for copy in outgoing:
        copy.wait()


def early_terms(width, *refs):
    kept = [refs[half * FIRST : (half + 1) * FIRST] for half in range(HALVES)]
    earlier, *refs = refs[HALVES * FIRST :]
    totals = refs[:HALVES]
    turn, fields, summed, sems, out_sems = refs[HALVES:]
    turn[...] = jnp.zeros_like(turn)
    edges = masks()
    copies = {}
    for half in range(HALVES):
        for tick in range(FIRST):
            copies[half, tick] = pltpu.make_async_copy(
                kept[half][tick], fields.at[half, tick], sems.at[half, tick]
            )
            copies[half, tick].start()
    outgoing = []
    for half in range(HALVES):
        for tick in range(FIRST):
            copies[half, tick].wait()
        for branch in range(2):
            for group in range(width // GW):
                lanes = group_lanes(group)
                planes = [
                    [fields[half, tick, branch, at, :, lanes] for tick in range(FIRST)]
                    for at in range(2)
                ]
                columns = [column_shifts(field.astype(jnp.float32), *edges) for field in planes[0]]
                rows = [row_shifts(field) for field in planes[1]]
                term = correlate(
                    jnp.concatenate(columns, axis=0), jnp.concatenate(rows, axis=0)
                ).astype(jnp.bfloat16)
                for a in range(3):
                    summed[half, branch, pl.ds(a * 3 * GW, 3 * GW), lanes] = term[
                        :, a * GW : (a + 1) * GW
                    ]
        copy = pltpu.make_async_copy(summed.at[half], totals[half], out_sems.at[half])
        copy.start()
        outgoing.append(copy)
    for copy in outgoing:
        copy.wait()


def last_tick(half, width, received, top, kernels, held, total, kept, earlier, *rest):
    if half:
        rest = rest[1:]
    made, final, mine, *rest = rest
    theirs, rest = rest[:2], rest[2:]
    groups = width // GW
    copies = []
    turn, *rest = rest
    if half + 1 < HALVES:
        following, summed, top_sem, final_sem, next_sems = rest
        copies += started(*kernel_copies(half + 1, width, kernels, following, next_sems)[::-1])
    else:
        summed, top_sem, final_sem = rest
    turn[...] = jnp.zeros_like(turn)
    take_state(TICKS - 1, half, width, received, top, made, top_sem)
    stacks = {}

    def weights(group, branch):
        return taps_by_row(held, branch, group_lanes(group))

    def keep(group, branch, columns, rows):
        stacks[group, branch] = columns, rows

    section_back(made, groups, weights, keep)
    copy = pltpu.make_async_copy(made, final.at[:, :, pl.ds(half * width, width)], final_sem)
    copy.start()
    copies.append(copy)
    edges = masks()
    z = lax.axis_index("dp_1")
    for branch in range(2):
        for group in range(groups):
            lanes = group_lanes(group)
            columns, rows = stacks[group, branch]
            early_columns = column_shifts(kept[branch, 0, :, lanes].astype(jnp.float32), *edges)
            term = correlate(
                jnp.concatenate([early_columns, columns], axis=0),
                jnp.concatenate([row_shifts(kept[branch, 1, :, lanes]), rows], axis=0),
            )
            for a in range(3):
                at = pl.ds(a * 3 * GW, 3 * GW)
                summed[branch, at, lanes] = (
                    total[branch, at, lanes].astype(jnp.float32) + term[:, a * GW : (a + 1) * GW]
                ).astype(jnp.bfloat16)
        for slot, block in enumerate(share_blocks(branch)):
            for z_slot in range(2):
                first = pl.multiple_of((2 * block + (z ^ z_slot)) * SHARE, 16)
                share = summed[branch, pl.ds(first, SHARE), :]
                if slot < 2:
                    mine[branch, slot, z_slot] = share
                else:
                    theirs[branch][slot - 2, z_slot] = share
    for copy in copies:
        copy.wait()


ANY_REF = pl.BlockSpec(memory_space=pl.ANY)
VMEM_REF = pl.BlockSpec(memory_space=pltpu.VMEM)


def in_vmem(array):
    return pltpu.with_memory_space_constraint(array, pltpu.VMEM)


def in_hbm(array):
    return pltpu.with_memory_space_constraint(array, pltpu.HBM)


def params():
    return pltpu.CompilerParams(vmem_limit_bytes=VMEM_LIMIT)


def cost(products, width):
    groups = width // GW
    return pl.CostEstimate(
        flops=products * 2 * CELLS * ROWS * GW * groups,
        bytes_accessed=4 * 4 * CELLS * width,
        transcendentals=2 * CELLS * width,
    )


def passed_down(value):
    count = lax.axis_size("section")
    return lax.ppermute(value, "section", [(source, source - 1) for source in range(1, count)])


def partners(branch, x):
    return (x ^ 1, 3 - x) if branch == 0 else (3 - x, x ^ 1)


def share_blocks(branch):
    x = lax.axis_index("dp_0")
    first, second = partners(branch, x)
    return x, second, first, partners(branch, first)[1]


def first_sum(mine, *refs):
    came, refs = refs[:2], refs[2:]
    earlier, passed, turn = refs[0], refs[1:3], refs[3]
    turn[...] = jnp.zeros_like(turn)
    for branch in range(2):
        passed[branch][...] = (
            mine[branch, 1].astype(jnp.float32) + came[branch][1].astype(jnp.float32)
        ).astype(jnp.bfloat16)


def second_sum(mine, *refs):
    came, came_next, refs = refs[:2], refs[2:4], refs[4:]
    earlier, across, kept, turn = refs
    turn[...] = jnp.zeros_like(turn)
    for branch in range(2):
        total = [
            mine[branch, 0, z_slot].astype(jnp.float32)
            + came[branch][0, z_slot].astype(jnp.float32)
            + came_next[branch][z_slot].astype(jnp.float32)
            for z_slot in range(2)
        ]
        kept[branch] = total[0]
        across[branch] = total[1].astype(jnp.bfloat16)


def last_sum(*refs):
    kept, came, out = refs[:HALVES], refs[HALVES:-1], refs[-1]
    for half in range(HALVES):
        width = kept[half].shape[-1]
        out[:, :, pl.ds(half * width, width)] = (
            kept[half][...] + came[half][...].astype(jnp.float32)
        ) * (1.0 / (HW * HW))


def summed_shares(mine, theirs, turn):
    width = mine[0].shape[-1]
    turn_type = pltpu.VMEM((8, 128), jnp.float32)
    halves = range(HALVES)
    pairs = [
        [[(x, partners(branch, x)[step]) for x in range(4)] for step in range(2)]
        for branch in range(2)
    ]
    passed_type = pltpu.VMEM((2, SHARE, width), jnp.bfloat16)
    came = [
        [in_vmem(lax.ppermute(theirs[half][b], "dp_0", pairs[b][0])) for b in range(2)]
        for half in halves
    ]
    came_next, came_last, kept = [], [], []
    for half in halves:
        *passed, turn = pl.pallas_call(
            first_sum,
            out_shape=(passed_type, passed_type, turn_type),
            in_specs=[VMEM_REF] * 3 + [ANY_REF],
            out_specs=(VMEM_REF,) * 3,
            compiler_params=params(),
            name=f"first_sum_{half}",
        )(mine[half], *came[half], turn)
        came_next.append(
            [in_vmem(lax.ppermute(passed[b], "dp_0", pairs[b][1])) for b in range(2)]
        )
    for half in halves:
        across, own, turn = pl.pallas_call(
            second_sum,
            out_shape=(passed_type, pltpu.VMEM((2, SHARE, width), jnp.float32), turn_type),
            in_specs=[VMEM_REF] * 5 + [ANY_REF],
            out_specs=(VMEM_REF, VMEM_REF, VMEM_REF),
            compiler_params=params(),
            name=f"second_sum_{half}",
        )(mine[half], *came[half], *came_next[half], turn)
        came_last.append(lax.ppermute(across, "dp_1", [(0, 1), (1, 0)]))
        kept.append(own)
    return pl.pallas_call(
        last_sum,
        out_shape=jax.ShapeDtypeStruct((2, SHARE, width * HALVES), jnp.float32),
        in_specs=[VMEM_REF] * (2 * HALVES),
        out_specs=VMEM_REF,
        compiler_params=params(),
        name="last_sum",
    )(*[in_vmem(own) for own in kept], *[in_vmem(part) for part in came_last])


def on_device(section_states, conv_kernels, top_feed):
    chans = section_states.shape[-1]
    width = chans // HALVES
    states = in_hbm(section_states.reshape(4, CELLS, chans))
    kernels = in_hbm(conv_kernels[0])
    top = in_hbm(top_feed.reshape(TICKS - 1, 4, CELLS, chans))

    groups = width // GW
    state_type = pltpu.VMEM((4, CELLS, width), jnp.bfloat16)
    kept_type = pltpu.HBM((2, 2, CELLS, width), jnp.bfloat16)
    held_type = pltpu.VMEM((2, ROWS, width), jnp.bfloat16)
    turn_type = pltpu.VMEM((8, 128), jnp.float32)
    dma = pltpu.SemaphoreType.DMA
    kept_scratch = pltpu.VMEM((2, 2, CELLS, width), jnp.bfloat16)
    turn = jnp.zeros((8, 128), jnp.float32)
    held = None
    made, kept = [None] * HALVES, [[] for _ in range(HALVES)]
    for tick in range(TICKS - 1):
        for half in range(HALVES):
            if (tick, half) == (FIRST, 0):
                *total, turn = pl.pallas_call(
                    functools.partial(early_terms, width),
                    out_shape=(
                        *[pltpu.HBM((2, ROWS, width), jnp.bfloat16) for _ in range(HALVES)],
                        turn_type,
                    ),
                    in_specs=[ANY_REF] * (HALVES * FIRST + 1),
                    out_specs=(*[ANY_REF] * HALVES, VMEM_REF),
                    scratch_shapes=[
                        pltpu.VMEM((HALVES, FIRST, 2, 2, CELLS, width), jnp.bfloat16),
                        pltpu.VMEM((HALVES, 2, ROWS, width), jnp.bfloat16),
                        dma((HALVES, FIRST)),
                        dma((HALVES,)),
                    ],
                    compiler_params=params(),
                    cost_estimate=cost(2 * FIRST * HALVES, width),
                    name="early_terms",
                )(*[in_hbm(plane) for side in kept for plane in side], turn)
            aliases = {}
            scratch = [kept_scratch, dma((2,)), dma(()), dma((2,))]
            if tick:
                operands = [in_vmem(made[half]), top, kernels, held, turn]
                specs = [VMEM_REF, ANY_REF, ANY_REF, VMEM_REF, ANY_REF]
                aliases = {0: 0}
            elif half:
                operands = [states, kernels, held, turn]
                specs = [ANY_REF, ANY_REF, VMEM_REF, ANY_REF]
            else:
                operands, specs = [states, kernels, turn], [ANY_REF] * 3
                scratch += [held_type, dma((2,))]
            out, fields, turn, following = pl.pallas_call(
                functools.partial(early_tick, tick, half, width),
                out_shape=(state_type, kept_type, turn_type, held_type),
                in_specs=specs,
                out_specs=(VMEM_REF, ANY_REF, VMEM_REF, VMEM_REF),
                scratch_shapes=scratch,
                input_output_aliases=aliases,
                compiler_params=params(),
                cost_estimate=cost(4, width),
                name=f"tick_{tick}_{half}",
            )(*operands)
            held = in_vmem(following)
            made[half] = passed_down(out)
            kept[half].append(fields)

    final = None
    mine, theirs = [None] * HALVES, [None] * HALVES
    theirs_type = pltpu.VMEM((2, 2, SHARE, width), jnp.bfloat16)
    for half in range(HALVES):
        operands = [in_vmem(made[half]), top, kernels, held, total[half], kept[half][FIRST], turn]
        specs = [VMEM_REF, ANY_REF, ANY_REF, VMEM_REF, VMEM_REF, VMEM_REF, ANY_REF]
        aliases = {0: 0}
        if half:
            aliases[len(operands)] = 1
            operands.append(in_hbm(final))
            specs.append(ANY_REF)
        more = half + 1 < HALVES
        _, final, mine[half], *theirs[half], turn = pl.pallas_call(
            functools.partial(last_tick, half, width),
            out_shape=(
                state_type,
                pltpu.HBM((4, CELLS, chans), jnp.bfloat16),
                pltpu.VMEM((2, 2, 2, SHARE, width), jnp.bfloat16),
                theirs_type,
                theirs_type,
                turn_type,
                *[held_type] * more,
            ),
            in_specs=specs,
            out_specs=(VMEM_REF, ANY_REF, *[VMEM_REF] * (4 + more)),
            scratch_shapes=[
                pltpu.VMEM((2, ROWS, width), jnp.bfloat16),
                dma(()),
                dma(()),
                *[dma((2,))] * more,
            ],
            input_output_aliases=aliases,
            compiler_params=params(),
            cost_estimate=cost(6, width),
            name=f"last_tick_{half}",
        )(*operands)
        if more:
            held = in_vmem(turn)
            *theirs[half], turn = theirs[half]
    grads = summed_shares(mine, theirs, turn)
    return (final.reshape(1, 4, 1, HW, HW, chans), grads[None])


def solution(mesh):
    finer = Mesh(mesh.devices.reshape(mesh.shape["section"], 4, 2), ("section", "dp_0", "dp_1"))
    images = ("dp_0", "dp_1")
    in_specs = (
        P("section", None, images, None, None, None),
        P("section", None, None, None),
        P(None, None, images, None, None, None),
    )
    out_specs = (P("section", None, images, None, None, None), P("section", None, images, None))
    return jax.shard_map(
        on_device, mesh=finer, in_specs=in_specs, out_specs=out_specs, check_vma=False
    )
```

```python
import functools

import jax
import jax.numpy as jnp
from jax import lax
from jax.experimental import pallas as pl
from jax.experimental.pallas import tpu as pltpu
from jax.sharding import Mesh
from jax.sharding import PartitionSpec as P

GW = 128
HW = 16
TICKS = 4
CELLS = HW * HW
ROWS = 9 * GW
SHARE = ROWS // 8
HALVES = 2
FIRST = TICKS - 2
VMEM_LIMIT = 24 * 1024 * 1024


def column_shifts(field, at_left, at_right):
    before = jnp.where(at_left, 0.0, pltpu.roll(field, 1, 0))
    after = jnp.where(at_right, 0.0, pltpu.roll(field, CELLS - 1, 0))
    return jnp.concatenate(
        [before.astype(jnp.bfloat16), field.astype(jnp.bfloat16), after.astype(jnp.bfloat16)], axis=1
    )


def row_shifts(field):
    edge = jnp.zeros((HW, GW), field.dtype)
    up = jnp.concatenate([field[HW:], edge], axis=0)
    down = jnp.concatenate([edge, field[:-HW]], axis=0)
    return jnp.concatenate([up, field, down], axis=1)


def taps_by_row(kernel_ref, branch, lanes):
    return jnp.concatenate(
        [kernel_ref[branch, pl.ds(a * 3 * GW, 3 * GW), lanes] for a in range(3)], axis=1
    )


def conv(stack, kernel):
    parts = jnp.dot(stack, kernel, preferred_element_type=jnp.float32)
    edge = jnp.zeros((HW, GW), jnp.float32)
    above = jnp.concatenate([edge, parts[:-HW, :GW]], axis=0)
    below = jnp.concatenate([parts[HW:, 2 * GW :], edge], axis=0)
    return parts[:, GW : 2 * GW] + above + below


def conv_back(stack, kernel, at_left, at_right):
    parts = lax.dot_general(
        stack, kernel, (((1,), (1,)), ((), ())), preferred_element_type=jnp.float32
    )
    before = jnp.where(at_right, 0.0, pltpu.roll(parts[:, :GW], CELLS - 1, 0))
    after = jnp.where(at_left, 0.0, pltpu.roll(parts[:, 2 * GW :], 1, 0))
    return parts[:, GW : 2 * GW] + before + after


def correlate(columns, rows):
    return lax.dot_general(
        columns, rows, (((0,), (0,)), ((), ())), preferred_element_type=jnp.float32
    )


def masks():
    column = lax.rem(lax.broadcasted_iota(jnp.int32, (CELLS, GW), 0), HW)
    return column == 0, column == HW - 1


def masks():
    column = lax.rem(lax.broadcasted_iota(jnp.int32, (CELLS, GW), 0), HW)
    return column == 0, column == HW - 1


def group_lanes(group):
    return pl.ds(group * GW, GW)


def first_branch(state_ref, lanes, weights, keep):
    edges = masks()
    grad_two = state_ref[3, :, lanes]
    out_one = state_ref[0, :, lanes].astype(jnp.float32)
    sigma = jax.nn.sigmoid(out_one)
    slope = sigma * (1.0 + out_one * (1.0 - sigma))
    columns = column_shifts(out_one * sigma, *edges)
    rows = row_shifts(grad_two)
    keep(1, columns, rows)
    weights = weights()
    in_two = (state_ref[1, :, lanes].astype(jnp.float32) - conv(columns, weights)).astype(
        jnp.bfloat16
    )
    total_one = (
        state_ref[2, :, lanes].astype(jnp.float32) + conv_back(rows, weights, *edges) * slope
    ).astype(jnp.bfloat16)
    return in_two, total_one


def second_branch(state_ref, lanes, weights, in_two, total_one, keep):
    edges = masks()
    wide_two = in_two.astype(jnp.float32)
    sigma = jax.nn.sigmoid(wide_two)
    slope = sigma * (1.0 + wide_two * (1.0 - sigma))
    columns = column_shifts(wide_two * sigma, *edges)
    rows = row_shifts(total_one)
    keep(0, columns, rows)
    weights = weights()
    out_one = state_ref[0, :, lanes].astype(jnp.float32)
    grad_two = state_ref[3, :, lanes].astype(jnp.float32)
    state_ref[0, :, lanes] = (out_one - conv(columns, weights)).astype(jnp.bfloat16)
    state_ref[1, :, lanes] = in_two
    state_ref[2, :, lanes] = total_one
    state_ref[3, :, lanes] = (grad_two + conv_back(rows, weights, *edges) * slope).astype(
        jnp.bfloat16
    )


def section_back(state_ref, groups, weights, keep):
    halfway = [
        first_branch(
            state_ref,
            group_lanes(group),
            functools.partial(weights, group, 1),
            functools.partial(keep, group),
        )
        for group in range(groups)
    ]
    for group in range(groups):
        second_branch(
            state_ref,
            group_lanes(group),
            functools.partial(weights, group, 0),
            *halfway[group],
            functools.partial(keep, group),
        )


def take_state(tick, half, width, received, top, made, sem):
    is_top = lax.axis_index("section") == lax.axis_size("section") - 1

    @pl.when(is_top)
    def _():
        copy = pltpu.make_async_copy(
            top.at[tick - 1, :, :, pl.ds(half * width, width)], made, sem
        )
        copy.start()
        copy.wait()

    @pl.when(jnp.logical_not(is_top))
    def _():
        made[...] = received[...]


def started(*copies):
    for copy in copies:
        copy.start()
    return list(copies)


def kernel_copies(half, width, kernels, held, sems):
    wide = pl.ds(half * width, width)
    return [
        pltpu.make_async_copy(kernels.at[branch, :, wide], held.at[branch], sems.at[branch])
        for branch in range(2)
    ]


def early_tick(tick, half, width, *refs):
    groups = width // GW
    loads, outgoing = [], []
    if tick == 0:
        states, kernels, *refs = refs
        if half:
            held, *refs = refs
        earlier, made, kept, turn, following, sent, out_sems, state_sem, next_sems, *refs = refs
        (state_load,) = started(
            pltpu.make_async_copy(states.at[:, :, pl.ds(half * width, width)], made, state_sem)
        )
        if not half:
            held, sems = refs
            loads = kernel_copies(half, width, kernels, held, sems)
            started(*loads[::-1])
    else:
        received, top, kernels, held, earlier, made, kept, turn, following, *refs = refs
        sent, out_sems, top_sem, next_sems = refs
    outgoing += started(
        *kernel_copies((half + 1) % HALVES, width, kernels, following, next_sems)[::-1]
    )
    turn[...] = jnp.zeros_like(turn)
    if tick:
        take_state(tick, half, width, received, top, made, top_sem)
    else:
        state_load.wait()

    def weights(group, branch):
        if group == 0 and loads:
            loads[branch].wait()
        return taps_by_row(held, branch, group_lanes(group))

    def keep(group, branch, columns, rows):
        lanes = group_lanes(group)
        sent[branch, 0, :, lanes] = columns[:, GW : 2 * GW]
        sent[branch, 1, :, lanes] = rows[:, GW : 2 * GW]
        if group == groups - 1:
            outgoing.extend(
                started(pltpu.make_async_copy(sent.at[branch], kept.at[branch], out_sems.at[branch]))
            )

    section_back(made, groups, weights, keep)
    for copy in outgoing:
        copy.wait()


def early_terms(width, *refs):
    kept = [refs[half * FIRST : (half + 1) * FIRST] for half in range(HALVES)]
    earlier, *refs = refs[HALVES * FIRST :]
    totals = refs[:HALVES]
    turn, fields, summed, sems, out_sems = refs[HALVES:]
    turn[...] = jnp.zeros_like(turn)
    edges = masks()
    copies = {}
    for half in range(HALVES):
        for tick in range(FIRST):
            copies[half, tick] = pltpu.make_async_copy(
                kept[half][tick], fields.at[half, tick], sems.at[half, tick]
            )
            copies[half, tick].start()
    outgoing = []
    for half in range(HALVES):
        for tick in range(FIRST):
            copies[half, tick].wait()
        for branch in range(2):
            for group in range(width // GW):
                lanes = group_lanes(group)
                planes = [
                    [fields[half, tick, branch, at, :, lanes] for tick in range(FIRST)]
                    for at in range(2)
                ]
                columns = [column_shifts(field.astype(jnp.float32), *edges) for field in planes[0]]
                rows = [row_shifts(field) for field in planes[1]]
                term = correlate(
                    jnp.concatenate(columns, axis=0), jnp.concatenate(rows, axis=0)
                ).astype(jnp.bfloat16)
                for a in range(3):
                    summed[half, branch, pl.ds(a * 3 * GW, 3 * GW), lanes] = term[
                        :, a * GW : (a + 1) * GW
                    ]
        copy = pltpu.make_async_copy(summed.at[half], totals[half], out_sems.at[half])
        copy.start()
        outgoing.append(copy)
    for copy in outgoing:
        copy.wait()


def last_tick(half, width, received, top, kernels, held, total, kept, earlier, *rest):
    if half:
        rest = rest[1:]
    made, final, mine, *rest = rest
    theirs, rest = rest[:2], rest[2:]
    groups = width // GW
    copies = []
    turn, *rest = rest
    if half + 1 < HALVES:
        following, summed, top_sem, final_sem, next_sems = rest
        copies += started(*kernel_copies(half + 1, width, kernels, following, next_sems)[::-1])
    else:
        summed, top_sem, final_sem = rest
    turn[...] = jnp.zeros_like(turn)
    take_state(TICKS - 1, half, width, received, top, made, top_sem)
    stacks = {}

    def weights(group, branch):
        return taps_by_row(held, branch, group_lanes(group))

    def keep(group, branch, columns, rows):
        stacks[group, branch] = columns, rows

    section_back(made, groups, weights, keep)
    copy = pltpu.make_async_copy(made, final.at[:, :, pl.ds(half * width, width)], final_sem)
    copy.start()
    copies.append(copy)
    edges = masks()
    z = lax.axis_index("dp_1")
    for branch in range(2):
        for group in range(groups):
            lanes = group_lanes(group)
            columns, rows = stacks[group, branch]
            early_columns = column_shifts(kept[branch, 0, :, lanes].astype(jnp.float32), *edges)
            term = correlate(
                jnp.concatenate([early_columns, columns], axis=0),
                jnp.concatenate([row_shifts(kept[branch, 1, :, lanes]), rows], axis=0),
            )
            for a in range(3):
                at = pl.ds(a * 3 * GW, 3 * GW)
                summed[branch, at, lanes] = (
                    total[branch, at, lanes].astype(jnp.float32) + term[:, a * GW : (a + 1) * GW]
                ).astype(jnp.bfloat16)
        for slot, block in enumerate(share_blocks(branch)):
            for z_slot in range(2):
                first = pl.multiple_of((2 * block + (z ^ z_slot)) * SHARE, 16)
                share = summed[branch, pl.ds(first, SHARE), :]
                if slot < 2:
                    mine[branch, slot, z_slot] = share
                else:
                    theirs[branch][slot - 2, z_slot] = share
    for copy in copies:
        copy.wait()


ANY_REF = pl.BlockSpec(memory_space=pl.ANY)
VMEM_REF = pl.BlockSpec(memory_space=pltpu.VMEM)


def in_vmem(array):
    return pltpu.with_memory_space_constraint(array, pltpu.VMEM)


def in_hbm(array):
    return pltpu.with_memory_space_constraint(array, pltpu.HBM)


def params():
    return pltpu.CompilerParams(vmem_limit_bytes=VMEM_LIMIT)


def cost(products, width):
    groups = width // GW
    return pl.CostEstimate(
        flops=products * 2 * CELLS * ROWS * GW * groups,
        bytes_accessed=4 * 4 * CELLS * width,
        transcendentals=2 * CELLS * width,
    )


def passed_down(value):
    count = lax.axis_size("section")
    return lax.ppermute(value, "section", [(source, source - 1) for source in range(1, count)])


def partners(branch, x):
    return (x ^ 1, 3 - x) if branch == 0 else (3 - x, x ^ 1)


def share_blocks(branch):
    x = lax.axis_index("dp_0")
    first, second = partners(branch, x)
    return x, second, first, partners(branch, first)[1]


def first_sum(mine, *refs):
    came, refs = refs[:2], refs[2:]
    earlier, passed, turn = refs[0], refs[1:3], refs[3]
    turn[...] = jnp.zeros_like(turn)
    for branch in range(2):
        passed[branch][...] = (
            mine[branch, 1].astype(jnp.float32) + came[branch][1].astype(jnp.float32)
        ).astype(jnp.bfloat16)


def second_sum(mine, *refs):
    came, came_next, refs = refs[:2], refs[2:4], refs[4:]
    earlier, across, kept, turn = refs
    turn[...] = jnp.zeros_like(turn)
    for branch in range(2):
        total = [
            mine[branch, 0, z_slot].astype(jnp.float32)
            + came[branch][0, z_slot].astype(jnp.float32)
            + came_next[branch][z_slot].astype(jnp.float32)
            for z_slot in range(2)
        ]
        kept[branch] = total[0]
        across[branch] = total[1].astype(jnp.bfloat16)


def last_sum(half, kept, came, before, out, total, sem):
    width = kept.shape[-1]
    total[...] = (kept[...] + came[...].astype(jnp.float32)) * (1.0 / (HW * HW))
    copy = pltpu.make_async_copy(total, out.at[:, :, pl.ds(half * width, width)], sem)
    copy.start()
    copy.wait()


def summed_shares(mine, theirs, turn):
    width = mine[0].shape[-1]
    turn_type = pltpu.VMEM((8, 128), jnp.float32)
    halves = range(HALVES)
    pairs = [
        [[(x, partners(branch, x)[step]) for x in range(4)] for step in range(2)]
        for branch in range(2)
    ]
    passed_type = pltpu.VMEM((2, SHARE, width), jnp.bfloat16)
    came = [
        [in_vmem(lax.ppermute(theirs[half][b], "dp_0", pairs[b][0])) for b in range(2)]
        for half in halves
    ]
    came_next, came_last, kept = [], [], []
    for half in halves:
        *passed, turn = pl.pallas_call(
            first_sum,
            out_shape=(passed_type, passed_type, turn_type),
            in_specs=[VMEM_REF] * 3 + [ANY_REF],
            out_specs=(VMEM_REF,) * 3,
            compiler_params=params(),
            name=f"first_sum_{half}",
        )(mine[half], *came[half], turn)
        came_next.append(
            [in_vmem(lax.ppermute(passed[b], "dp_0", pairs[b][1])) for b in range(2)]
        )
    for half in halves:
        across, own, turn = pl.pallas_call(
            second_sum,
            out_shape=(passed_type, pltpu.VMEM((2, SHARE, width), jnp.float32), turn_type),
            in_specs=[VMEM_REF] * 5 + [ANY_REF],
            out_specs=(VMEM_REF, VMEM_REF, VMEM_REF),
            compiler_params=params(),
            name=f"second_sum_{half}",
        )(mine[half], *came[half], *came_next[half], turn)
        came_last.append(lax.ppermute(across, "dp_1", [(0, 1), (1, 0)]))
        kept.append(own)
    out = turn
    for half in halves:
        out = pl.pallas_call(
            functools.partial(last_sum, half),
            out_shape=pltpu.HBM((2, SHARE, width * HALVES), jnp.float32),
            in_specs=[VMEM_REF, VMEM_REF, ANY_REF],
            out_specs=ANY_REF,
            scratch_shapes=[
                pltpu.VMEM((2, SHARE, width), jnp.float32),
                pltpu.SemaphoreType.DMA(()),
            ],
            input_output_aliases={2: 0} if half else {},
            compiler_params=params(),
            name=f"last_sum_{half}",
        )(in_vmem(kept[half]), in_vmem(came_last[half]), in_hbm(out) if half else out)
    return out


def on_device(section_states, conv_kernels, top_feed):
    chans = section_states.shape[-1]
    width = chans // HALVES
    states = in_hbm(section_states.reshape(4, CELLS, chans))
    kernels = in_hbm(conv_kernels[0])
    top = in_hbm(top_feed.reshape(TICKS - 1, 4, CELLS, chans))

    groups = width // GW
    state_type = pltpu.VMEM((4, CELLS, width), jnp.bfloat16)
    kept_type = pltpu.HBM((2, 2, CELLS, width), jnp.bfloat16)
    held_type = pltpu.VMEM((2, ROWS, width), jnp.bfloat16)
    turn_type = pltpu.VMEM((8, 128), jnp.float32)
    dma = pltpu.SemaphoreType.DMA
    kept_scratch = pltpu.VMEM((2, 2, CELLS, width), jnp.bfloat16)
    turn = jnp.zeros((8, 128), jnp.float32)
    held = None
    made, kept = [None] * HALVES, [[] for _ in range(HALVES)]
    for tick in range(TICKS - 1):
        for half in range(HALVES):
            if (tick, half) == (FIRST, 0):
                *total, turn = pl.pallas_call(
                    functools.partial(early_terms, width),
                    out_shape=(
                        *[pltpu.HBM((2, ROWS, width), jnp.bfloat16) for _ in range(HALVES)],
                        turn_type,
                    ),
                    in_specs=[ANY_REF] * (HALVES * FIRST + 1),
                    out_specs=(*[ANY_REF] * HALVES, VMEM_REF),
                    scratch_shapes=[
                        pltpu.VMEM((HALVES, FIRST, 2, 2, CELLS, width), jnp.bfloat16),
                        pltpu.VMEM((HALVES, 2, ROWS, width), jnp.bfloat16),
                        dma((HALVES, FIRST)),
                        dma((HALVES,)),
                    ],
                    compiler_params=params(),
                    cost_estimate=cost(2 * FIRST * HALVES, width),
                    name="early_terms",
                )(*[in_hbm(plane) for side in kept for plane in side], turn)
            aliases = {}
            scratch = [kept_scratch, dma((2,)), dma(()), dma((2,))]
            if tick:
                operands = [in_vmem(made[half]), top, kernels, held, turn]
                specs = [VMEM_REF, ANY_REF, ANY_REF, VMEM_REF, ANY_REF]
                aliases = {0: 0}
            elif half:
                operands = [states, kernels, held, turn]
                specs = [ANY_REF, ANY_REF, VMEM_REF, ANY_REF]
            else:
                operands, specs = [states, kernels, turn], [ANY_REF] * 3
                scratch += [held_type, dma((2,))]
            out, fields, turn, following = pl.pallas_call(
                functools.partial(early_tick, tick, half, width),
                out_shape=(state_type, kept_type, turn_type, held_type),
                in_specs=specs,
                out_specs=(VMEM_REF, ANY_REF, VMEM_REF, VMEM_REF),
                scratch_shapes=scratch,
                input_output_aliases=aliases,
                compiler_params=params(),
                cost_estimate=cost(4, width),
                name=f"tick_{tick}_{half}",
            )(*operands)
            held = in_vmem(following)
            made[half] = passed_down(out)
            kept[half].append(fields)

    final = None
    mine, theirs = [None] * HALVES, [None] * HALVES
    theirs_type = pltpu.VMEM((2, 2, SHARE, width), jnp.bfloat16)
    for half in range(HALVES):
        operands = [in_vmem(made[half]), top, kernels, held, total[half], kept[half][FIRST], turn]
        specs = [VMEM_REF, ANY_REF, ANY_REF, VMEM_REF, VMEM_REF, VMEM_REF, ANY_REF]
        aliases = {0: 0}
        if half:
            aliases[len(operands)] = 1
            operands.append(in_hbm(final))
            specs.append(ANY_REF)
        more = half + 1 < HALVES
        _, final, mine[half], *theirs[half], turn = pl.pallas_call(
            functools.partial(last_tick, half, width),
            out_shape=(
                state_type,
                pltpu.HBM((4, CELLS, chans), jnp.bfloat16),
                pltpu.VMEM((2, 2, 2, SHARE, width), jnp.bfloat16),
                theirs_type,
                theirs_type,
                turn_type,
                *[held_type] * more,
            ),
            in_specs=specs,
            out_specs=(VMEM_REF, ANY_REF, *[VMEM_REF] * (4 + more)),
            scratch_shapes=[
                pltpu.VMEM((2, ROWS, width), jnp.bfloat16),
                dma(()),
                dma(()),
                *[dma((2,))] * more,
            ],
            input_output_aliases=aliases,
            compiler_params=params(),
            cost_estimate=cost(6, width),
            name=f"last_tick_{half}",
        )(*operands)
        if more:
            held = in_vmem(turn)
            *theirs[half], turn = theirs[half]
    grads = summed_shares(mine, theirs, turn)
    return (final.reshape(1, 4, 1, HW, HW, chans), grads[None])


def solution(mesh):
    finer = Mesh(mesh.devices.reshape(mesh.shape["section"], 4, 2), ("section", "dp_0", "dp_1"))
    images = ("dp_0", "dp_1")
    in_specs = (
        P("section", None, images, None, None, None),
        P("section", None, None, None),
        P(None, None, images, None, None, None),
    )
    out_specs = (P("section", None, images, None, None, None), P("section", None, images, None))
    return jax.shard_map(
        on_device, mesh=finer, in_specs=in_specs, out_specs=out_specs, check_vma=False
    )
```
